256 devices in a mesh: gx: 8 (over y_lo, x), gy: 4 (over y_hi, core), gz: 8 (over z).
Axes of the slice: x: 4, y: 4 (y_hi: 2, y_lo: 2; y = y_hi * 2 + y_lo), z: 8, core: 2. Of those that a mesh axis runs over, the one named last changes fastest.
Arguments:
- density: float32 [256, 128, 2048], P('gx', 'gy', 'gz'), may hold values from 0 to 1
- voxel_kind: int32 [256, 128, 2048], P('gx', 'gy', 'gz'), may hold values from 0 to 3
- velocity: float32 [3, 256, 128, 2048], P(None, 'gx', 'gy', 'gz'), may hold values from -6 to 6
- adjoint: float32 [4, 256, 128, 2048], P(None, 'gx', 'gy', 'gz'), may hold values from -6 to 6
Outputs:
- adjoint_residual: float32 [4, 256, 128, 2048], P(None, 'gx', 'gy', 'gz')
- sensitivity: float32 [256, 128, 2048], P('gx', 'gy', 'gz')
The draws below stay inside these ranges and needn't reach their ends.
All inputs are finite; a program needn't handle non-finite values.
Results may differ from the reference program's by a relative error of at most 0.0003.
Values sent between devices are 32-bit elements; how exact they have to be, the bound alone decides.
A program may use at most 192 MiB of HBM per device.

```python
import math
import jax
import jax.numpy as jnp
from jax import lax

NX = 256
NY = 128
NZ = 2048


def wave_sum(key, comps, count):
    freq_key, sign_key, phase_key = jax.random.split(key, 3)
    wave_rates = jax.random.uniform(freq_key, (comps, count, 3), jnp.float32, 1.0 / 64.0, 1.0 / 20.0) * (2.0 * math.pi)
    sign_draw = jax.random.randint(sign_key, (comps, count, 3), 0, 2)
    wave_rates = wave_rates * jnp.where(sign_draw == 1, 1.0, -1.0)
    phase_shift = jax.random.uniform(phase_key, (comps, count), jnp.float32, -math.pi, math.pi)
    x_coord = jnp.arange(NX, dtype=jnp.float32)[:, None, None]
    y_coord = jnp.arange(NY, dtype=jnp.float32)[None, :, None]
    z_coord = jnp.arange(NZ, dtype=jnp.float32)[None, None, :]
    fields = []
    for c in range(comps):
        summed = jnp.zeros((NX, NY, NZ), jnp.float32)
        for m in range(count):
            angle_sum = wave_rates[c, m, 0] * x_coord + wave_rates[c, m, 1] * y_coord + wave_rates[c, m, 2] * z_coord + phase_shift[c, m]
            summed = summed + jnp.cos(angle_sum)
        fields.append(summed * math.sqrt(2.0 / count))
    return jnp.stack(fields, 0)


def draw_density(key, part):
    key = jax.random.fold_in(key, 5)
    mode_key, noise_key = jax.random.split(key)
    waves = wave_sum(mode_key, 1, 6)[0]
    rough = 0.8 * jnp.clip(jax.random.normal(noise_key, (NX, NY, NZ), jnp.float32), -4.0, 4.0)
    logit = 4.0 * waves + rough
    return jax.nn.sigmoid(logit).astype(jnp.float32)


def draw_velocity(key, part):
    key = jax.random.fold_in(key, 11)
    mode_key, noise_key = jax.random.split(key)
    waves = wave_sum(mode_key, 3, 6)
    rough = 0.25 * jnp.clip(jax.random.normal(noise_key, (3, NX, NY, NZ), jnp.float32), -4.0, 4.0)
    return (waves + rough).astype(jnp.float32)


def draw_adjoint(key, part):
    key = jax.random.fold_in(key, 13)
    mode_key, noise_key = jax.random.split(key)
    waves = wave_sum(mode_key, 4, 6)
    rough = 0.25 * jnp.clip(jax.random.normal(noise_key, (4, NX, NY, NZ), jnp.float32), -4.0, 4.0)
    return (waves + rough).astype(jnp.float32)


def draw_voxel_kind(key, part):
    key = jax.random.fold_in(key, 7)
    values = jax.random.randint(key, (NX, NY, NZ), 0, 20)
    kinds = jnp.where(values < 3, 1, jnp.where(values == 3, 2, jnp.where(values == 4, 3, 0)))
    return kinds.astype(jnp.int32)


def setup_inputs(seed: int = 0) -> dict:
    key_list = jax.random.split(jax.random.key(seed), 5)
    return {
        "density": draw_density(jax.random.fold_in(key_list[4], 71), 0),
        "voxel_kind": draw_voxel_kind(jax.random.fold_in(key_list[4], 71), 0),
        "velocity": draw_velocity(jax.random.fold_in(key_list[4], 71), 0),
        "adjoint": draw_adjoint(jax.random.fold_in(key_list[4], 71), 0),
    }


taps_list = [(7.0 - abs(k)) / 49.0 for k in range(-6, 7)]
proj_denom = 2.0 * math.tanh(2.0)


def smooth_axis(field, dim, count):
    total = jnp.zeros(field.shape[:dim] + (count,) + field.shape[dim + 1:], field.dtype)
    for k in range(13):
        total = total + taps_list[k] * lax.slice_in_dim(field, k, k + count, axis=dim)
    return total


def filter_field(field):
    padded = jnp.pad(field, 6)
    first = smooth_axis(padded, 0, field.shape[0])
    second = smooth_axis(first, 1, field.shape[1])
    return smooth_axis(second, 2, field.shape[2])


def stencils(padded):
    center = padded[..., 1:-1, 1:-1, 1:-1]
    xplus = padded[..., 2:, 1:-1, 1:-1]
    xminus = padded[..., :-2, 1:-1, 1:-1]
    yplus = padded[..., 1:-1, 2:, 1:-1]
    yminus = padded[..., 1:-1, :-2, 1:-1]
    zplus = padded[..., 1:-1, 1:-1, 2:]
    zminus = padded[..., 1:-1, 1:-1, :-2]
    laplace = xplus + xminus + yplus + yminus + zplus + zminus - 6.0 * center
    grads = ((xplus - xminus) * 0.5, (yplus - yminus) * 0.5, (zplus - zminus) * 0.5)
    return center, laplace, grads


def design_terms(rho_filt, voxel_kind, flow_pad, adj_pad):
    design = voxel_kind == 0
    solid = voxel_kind == 1
    inlet = voxel_kind == 2
    outlet = voxel_kind == 3
    tanh_part = jnp.tanh(4.0 * (rho_filt - 0.5))
    proj = (math.tanh(2.0) + tanh_part) / proj_denom
    rho_proj = jnp.where(design, proj, jnp.where(solid, 0.0, 1.0))
    alpha = 2.0 * (1.0 - rho_proj) / (1.0 + rho_proj)
    flow_c, flow_lap, unused_a = stencils(flow_pad)
    lam_c, lam_lap, lam_grads = stencils(adj_pad[:3])
    mu_c, unused_b, mu_grads = stencils(adj_pad[3])
    mu_grad = jnp.stack(mu_grads, 0)
    momentum = -lam_lap + alpha * lam_c - mu_grad + 2.0 * alpha * flow_c - 2.0 * flow_lap
    momentum = jnp.where(inlet, lam_c, momentum)
    div_lam = lam_grads[0][0] + lam_grads[1][1] + lam_grads[2][2]
    continuity = jnp.where(outlet, mu_c, -div_lam)
    residual = jnp.concatenate([momentum, continuity[None]], 0)
    d_alpha = -4.0 / ((1.0 + rho_proj) * (1.0 + rho_proj))
    d_proj = 4.0 * (1.0 - tanh_part * tanh_part) / proj_denom
    energy = jnp.sum(flow_c * flow_c, 0) + jnp.sum(flow_c * lam_c, 0)
    pointwise = jnp.where(design, d_alpha * energy * d_proj, 0.0)
    return residual, pointwise


def reference(density, voxel_kind, velocity, adjoint):
    rho_filt = filter_field(density)
    pad_spec = ((0, 0), (1, 1), (1, 1), (1, 1))
    flow_pad = jnp.pad(velocity, pad_spec)
    adj_pad = jnp.pad(adjoint, pad_spec)
    residual, pointwise = design_terms(rho_filt, voxel_kind, flow_pad, adj_pad)
    return residual, filter_field(pointwise)
```

```python
import math

import jax
import jax.numpy as jnp
from jax import lax
from jax.experimental import pallas as pl
from jax.experimental.pallas import tpu as pltpu
from jax.sharding import PartitionSpec as P

MESH = pl.DeviceIdType.MESH
NB = {"gx": 8, "gy": 4, "gz": 8}
X, Y, Z = 32, 32, 256
TANH2 = math.tanh(2.0)
CUBE = 1.0 / (49.0**3)

NAMES = (
    [f"a{c}{i}" for c in "yz" for i in (0, 1)]
    + [f"ad{i}{j}" for i in (0, 1) for j in (0, 1)]
    + [f"{c}{i}" for c in ("e", "bn", "bf", "fx", "fy", "fz", "dy", "dz") for i in (0, 1)]
    + [f"dd{i}{j}" for i in (0, 1) for j in (0, 1)]
)
SLOT = {n: i for i, n in enumerate(NAMES)}


def exists(offs):
    ok = None
    for axis, d in offs.items():
        i = lax.axis_index(axis)
        c = (i > 0) if d < 0 else (i < NB[axis] - 1)
        ok = c if ok is None else jnp.logical_and(ok, c)
    return ok


class Msg:
    def __init__(self, sems, name, offs, src, dst):
        self.offs = offs
        self.back = {a: -d for a, d in offs.items()}
        k = SLOT[name]
        self.copy = pltpu.make_async_remote_copy(
            src_ref=src,
            dst_ref=dst,
            send_sem=sems[0].at[k],
            recv_sem=sems[1].at[k],
            device_id={a: lax.axis_index(a) + d for a, d in offs.items()},
            device_id_type=MESH,
        )

    def start(self):
        @pl.when(exists(self.offs))
        def _():
            self.copy.start()

    def wait_recv(self):
        @pl.when(exists(self.back))
        def _():
            self.copy.wait_recv()

    def wait_send(self):
        @pl.when(exists(self.offs))
        def _():
            self.copy.wait_send()


def enter():
    barrier = pltpu.get_barrier_semaphore()
    total = jnp.int32(0)
    offs = [{a: d} for a in NB for d in (-1, 1)]
    offs += [{"gy": i, "gz": j} for i in (-1, 1) for j in (-1, 1)]
    for o in offs:
        c = exists(o)

        @pl.when(c)
        def _():
            pl.semaphore_signal(
                barrier, inc=1, device_id={a: lax.axis_index(a) + d for a, d in o.items()}, device_id_type=MESH
            )

        total = total + c.astype(jnp.int32)
    return barrier, total


def lanes(shape):
    return lax.broadcasted_iota(jnp.int32, shape, len(shape) - 1)


def rows(shape):
    return lax.broadcasted_iota(jnp.int32, shape, len(shape) - 2)


def y_filter(ref, *at):
    acc = 7.0 * ref[(*at, pl.ds(8, Y))]
    for k in range(1, 7):
        acc = acc + (7.0 - k) * (ref[(*at, pl.ds(8 - k, Y))] + ref[(*at, pl.ds(8 + k, Y))])
    return acc


def x_filter(ref, at):
    acc = 7.0 * ref[at + 6]
    for k in range(1, 7):
        acc = acc + (7.0 - k) * (ref[at + 6 - k] + ref[at + 6 + k])
    return acc


def split(v):
    hi = v.astype(jnp.bfloat16)
    lo = (v - hi.astype(jnp.float32)).astype(jnp.bfloat16)
    return jnp.concatenate([hi, lo], axis=0)


def pack_z(ref, first, out):
    slot = lanes((Y, 128)) // 8

    def pair(j, carry):
        left = jnp.zeros((Y, 128), jnp.float32)
        right = jnp.zeros((Y, 128), jnp.float32)
        for s in range(16):
            x = j * 16 + s
            a = ref[x, pl.ds(first, Y), 0:128]
            b = ref[x, pl.ds(first, Y), 128:256]
            a = a if s == 0 else pltpu.roll(a, 8 * s, 1)
            b = b if s == 15 else pltpu.roll(b, 8 * s + 8, 1)
            left = jnp.where(slot == s, a, left)
            right = jnp.where(slot == s, b, right)
        out[0, j] = left
        out[1, j] = right
        return carry

    lax.fori_loop(0, 2, pair, 0)


def y_strips(zx, zy):
    for side in (0, 1):
        for j in (0, 1):
            zy[side, j] = y_filter(zx, side, j)


def yz_group(ref, zy, band, edge, x0, put):
    lane = lanes((Y, 128))
    body = [y_filter(ref, x0 + i) for i in range(4)]
    ends = []
    for i in range(4):
        x = x0 + i
        s, j = x % 16, x // 16
        before = pltpu.roll(zy[0, j], 120 - 8 * s, 1)
        after = pltpu.roll(zy[1, j], 128 - 8 * s, 1)
        ends.append(jnp.where(lane < 64, after, before))
    full = split(jnp.concatenate(body, axis=0))
    tips = split(jnp.concatenate(ends, axis=0))
    res = jnp.dot(full, band[...], preferred_element_type=jnp.float32)
    res = res + jnp.dot(tips, edge[...], preferred_element_type=jnp.float32)
    res = res[: 4 * Y] + res[4 * Y :]
    for i in range(4):
        put(x0 + i, res[i * Y : (i + 1) * Y])


def y_up(v):
    return jnp.where(rows(v.shape) == Y - 1, 0.0, pltpu.roll(v, Y - 1, 0))


def y_dn(v):
    return jnp.where(rows(v.shape) == 0, 0.0, pltpu.roll(v, 1, 0))


def z_up(v):
    return jnp.where(lanes(v.shape) == Z - 1, 0.0, pltpu.roll(v, Z - 1, 1))


def z_dn(v):
    return jnp.where(lanes(v.shape) == 0, 0.0, pltpu.roll(v, 1, 1))


def kernel(
    den_h, kind_h, vel_h, adj_h, res_o, sen_o,
    den, kind, vel, adj, zp, zx, zy, zp2, zx2, filt, em, pw, alpha, grid, res, sen,
    cxs, cxr, cys, cyr, czs, czr, band, edge, send, recv, load,
):
    sems = (send, recv)
    ix, iy, iz = (lax.axis_index(a) for a in NB)
    loads = [
        pltpu.make_async_copy(den_h, den.at[:, pl.ds(8, Y), :], load.at[0]),
        pltpu.make_async_copy(vel_h, vel, load.at[1]),
        pltpu.make_async_copy(adj_h, adj, load.at[2]),
        pltpu.make_async_copy(kind_h, kind, load.at[3]),
    ]
    for c in loads:
        c.start()
    barrier, total = enter()

    @pl.when(ix == 0)
    def _():
        filt[0:12] = jnp.zeros((12, Y, Z), jnp.float32)
        em[0:6] = jnp.zeros((6, Y, Z), jnp.float32)
        cxr[0] = jnp.zeros((4, Y, Z), jnp.float32)

    @pl.when(ix == NB["gx"] - 1)
    def _():
        filt[44:56] = jnp.zeros((12, Y, Z), jnp.float32)
        em[38:44] = jnp.zeros((6, Y, Z), jnp.float32)
        cxr[1] = jnp.zeros((4, Y, Z), jnp.float32)

    @pl.when(iz == 0)
    def _():
        zx[0] = jnp.zeros((2, 48, 128), jnp.float32)
        zx2[0] = jnp.zeros((2, 48, 128), jnp.float32)
        czr[0] = jnp.zeros((Y, 128), jnp.float32)

    @pl.when(iz == NB["gz"] - 1)
    def _():
        zx[1] = jnp.zeros((2, 48, 128), jnp.float32)
        zx2[1] = jnp.zeros((2, 48, 128), jnp.float32)
        czr[1] = jnp.zeros((Y, 128), jnp.float32)

    for edge_at, first in ((0, 0), (NB["gy"] - 1, 40)):

        @pl.when(iy == edge_at)
        def _():
            for r in (zx, zx2):
                r[:, :, pl.ds(first, 8), :] = jnp.zeros((2, 2, 8, 128), jnp.float32)
            for r in (den, grid):
                r[:, pl.ds(first, 8), :] = jnp.zeros((X, 8, Z), jnp.float32)

    def clear(x, carry):
        for side in (0, 1):
            for c in range(4):
                cyr[side, c, x] = jnp.zeros((8, Z), jnp.float32)
        return carry

    lax.fori_loop(0, X, clear, 0)

    i, j = rows((Z, Z)), lanes((Z, Z))
    band[...] = jnp.maximum(7 - jnp.abs(i - j), 0).astype(jnp.float32).astype(jnp.bfloat16)
    i, j = rows((128, Z)), lanes((128, Z))
    i = jnp.where(i < 64, i + Z, i - 128)
    edge[...] = jnp.maximum(7 - jnp.abs(i - j), 0).astype(jnp.float32).astype(jnp.bfloat16)

    loads[0].wait()
    pack_z(den, 8, zp)
    pl.semaphore_wait(barrier, total)

    def yz_messages(name, src, packed, dst, strips, first):
        out = [
            Msg(sems, f"{name}y0", {"gy": -1}, src.at[:, pl.ds(first, 6), :], dst.at[:, pl.ds(40, 6), :]),
            Msg(sems, f"{name}y1", {"gy": 1}, src.at[:, pl.ds(first + 26, 6), :], dst.at[:, pl.ds(2, 6), :]),
            Msg(sems, f"{name}z0", {"gz": -1}, packed.at[0], strips.at[1, :, pl.ds(8, Y), :]),
            Msg(sems, f"{name}z1", {"gz": 1}, packed.at[1], strips.at[0, :, pl.ds(8, Y), :]),
        ]
        for a, (d, mine, there) in enumerate(((-1, 0, 40), (1, 26, 2))):
            for b, e in enumerate((-1, 1)):
                out.append(
                    Msg(
                        sems, f"{name}d{a}{b}", {"gy": d, "gz": e},
                        packed.at[b, :, pl.ds(mine, 6), :], strips.at[1 - b, :, pl.ds(there, 6), :],
                    )
                )
        return out

    msg_a = yz_messages("a", den, zp, den, zx, 8)
    for m in msg_a:
        m.start()

    for c in loads[1:]:
        c.wait()

    def energy(x, carry):
        e = None
        for d in range(3):
            u = vel[d, x]
            t = u * (u + adj[d, x])
            e = t if e is None else e + t
        em[x + 6] = jnp.where(kind[x] == 0, e, 0.0)
        return carry

    lax.fori_loop(0, X, energy, 0)
    msg_e = [
        Msg(sems, "e0", {"gx": -1}, em.at[6:12], em.at[38:44]),
        Msg(sems, "e1", {"gx": 1}, em.at[32:38], em.at[0:6]),
    ]
    for m in msg_e:
        m.start()

    lane = lanes((Y, 128))

    def stencil(x, carry, lower, upper):
        to_prev, to_next = carry
        lam = [adj[d, x] for d in range(3)]
        mu2 = adj[3, x] * 0.5
        w = [lam[d] + 2.0 * vel[d, x] for d in range(3)]
        plus = [w[d] + mu2 for d in range(3)]
        minus = [w[d] - mu2 for d in range(3)]

        def at(d, q):
            return adj[d, q] + 2.0 * vel[d, q]

        out = []
        for d in range(3):
            t = y_up(plus[1] if d == 1 else w[d]) + y_dn(minus[1] if d == 1 else w[d])
            t = t + z_up(plus[2] if d == 2 else w[d]) + z_dn(minus[2] if d == 2 else w[d])
            if lower:
                t = t + at(d, x - 1)
                if d == 0:
                    t = t - 0.5 * adj[3, x - 1]
            if upper:
                t = t + at(d, x + 1)
                if d == 0:
                    t = t + 0.5 * adj[3, x + 1]
            out.append(-t)
        div = y_up(lam[1]) - y_dn(lam[1]) + z_up(lam[2]) - z_dn(lam[2])
        if upper:
            div = div + adj[0, x + 1]
        if lower:
            div = div - adj[0, x - 1]
        out.append(-0.5 * div)
        for c in range(4):
            res[c, x] = out[c]

        if not lower:
            cxs[0, 0], cxs[0, 1], cxs[0, 2], cxs[0, 3] = -plus[0], -w[1], -w[2], -0.5 * lam[0]
        if not upper:
            cxs[1, 0], cxs[1, 1], cxs[1, 2], cxs[1, 3] = -minus[0], -w[1], -w[2], 0.5 * lam[0]
        for side, part, end, sign in ((0, plus, slice(0, 8), -0.5), (1, minus, slice(Y - 8, Y), 0.5)):
            cys[side, 0, x] = -w[0][end]
            cys[side, 1, x] = -part[1][end]
            cys[side, 2, x] = -w[2][end]
            cys[side, 3, x] = sign * lam[1][end]
        zs0 = (-w[0], -w[1], -plus[2], -0.5 * lam[2])
        zs1 = (-w[0], -w[1], -minus[2], 0.5 * lam[2])
        for c in range(4):
            at_lane = c * X + x
            first = pltpu.roll(zs0[c][:, 0:128], at_lane, 1)
            last = pltpu.roll(zs1[c][:, 128:256], lax.rem(at_lane + 1, 128), 1)
            to_prev = jnp.where(lane == at_lane, first, to_prev)
            to_next = jnp.where(lane == at_lane, last, to_next)
        return to_prev, to_next

    ends = (jnp.zeros((Y, 128), jnp.float32), jnp.zeros((Y, 128), jnp.float32))
    ends = stencil(0, ends, False, True)
    ends = lax.fori_loop(1, X - 1, lambda x, c: stencil(x, c, True, True), ends)
    ends = stencil(X - 1, ends, True, False)
    czs[0], czs[1] = ends

    msg_f = [
        Msg(sems, "fx0", {"gx": -1}, cxs.at[0], cxr.at[1]),
        Msg(sems, "fx1", {"gx": 1}, cxs.at[1], cxr.at[0]),
        Msg(sems, "fy0", {"gy": -1}, cys.at[0, :, :, 0:1, :], cyr.at[1, :, :, 7:8, :]),
        Msg(sems, "fy1", {"gy": 1}, cys.at[1, :, :, 7:8, :], cyr.at[0, :, :, 0:1, :]),
        Msg(sems, "fz0", {"gz": -1}, czs.at[0], czr.at[1]),
        Msg(sems, "fz1", {"gz": 1}, czs.at[1], czr.at[0]),
    ]

    for m in msg_a:
        m.wait_recv()
    y_strips(zx, zy)

    def put_filt(x, v):
        filt[x + 12] = v

    def outer(g, carry):
        yz_group(den, zy, band, edge, g * 4, put_filt)
        yz_group(den, zy, band, edge, 20 + g * 4, put_filt)
        return carry

    lax.fori_loop(0, 3, outer, 0)
    msg_b = [
        Msg(sems, "bn0", {"gx": -1}, filt.at[12:18], filt.at[44:50]),
        Msg(sems, "bn1", {"gx": 1}, filt.at[38:44], filt.at[6:12]),
        Msg(sems, "bf0", {"gx": -1}, filt.at[18:24], filt.at[50:56]),
        Msg(sems, "bf1", {"gx": 1}, filt.at[32:38], filt.at[0:6]),
    ]
    for m in msg_b:
        m.start()
    for m in msg_f:
        m.start()
    for g in (12, 16):
        yz_group(den, zy, band, edge, g, put_filt)

    def project(e):
        t = jnp.tanh(x_filter(filt, e) * (4.0 * CUBE) - 2.0)
        r = 1.0 / (1.0 + (TANH2 + t) * (0.5 / TANH2))
        pw[e] = (-8.0 / TANH2) * (r * r) * (1.0 - t * t) * em[e]
        return r

    def project_own(x, carry):
        r = project(x + 6)
        k = kind[x]
        alpha[x] = jnp.where(k == 0, 4.0 * r - 2.0, jnp.where(k == 1, 2.0, 0.0))
        return carry

    def project_halo(e, carry):
        project(e)
        return carry

    def smooth_x(x, carry):
        grid[x, pl.ds(8, Y), :] = x_filter(pw, x)
        return carry

    lax.fori_loop(6, 26, project_own, 0)
    for m in msg_b[:2]:
        m.wait_recv()
    for lo, hi in ((0, 6), (26, 32)):
        lax.fori_loop(lo, hi, project_own, 0)
    lax.fori_loop(6, 26, smooth_x, 0)
    for m in msg_e:
        m.wait_recv()
    for m in msg_b[2:]:
        m.wait_recv()
    for lo, hi in ((0, 6), (38, 44)):
        lax.fori_loop(lo, hi, project_halo, 0)
    for lo, hi in ((0, 6), (26, 32)):
        lax.fori_loop(lo, hi, smooth_x, 0)

    pack_z(grid, 8, zp2)
    msg_d = yz_messages("d", grid, zp2, grid, zx2, 8)
    for m in msg_d:
        m.start()

    for m in msg_f:
        m.wait_recv()
    for c in range(4):
        res[c, 0] += cxr[0, c]
        res[c, X - 1] += cxr[1, c]

    def finish(x, carry):
        a = alpha[x] + 6.0
        k = kind[x]
        for c in range(4):
            at_lane = c * X + x
            first = pltpu.roll(czr[0], lax.rem(128 - at_lane, 128), 1)
            last = pltpu.roll(czr[1], 127 - at_lane, 1)
            res[c, x, 0:8] += cyr[0, c, x]
            res[c, x, Y - 8 : Y] += cyr[1, c, x]
            r = res[c, x] + jnp.concatenate([jnp.where(lane == 0, first, 0.0), jnp.where(lane == 127, last, 0.0)], axis=1)
            v = adj[c, x]
            if c < 3:
                res[c, x] = jnp.where(k == 2, v, r + a * (v + 2.0 * vel[c, x]))
            else:
                res[c, x] = jnp.where(k == 3, v, r)
        return carry

    lax.fori_loop(0, X, finish, 0)
    out_r = pltpu.make_async_copy(res, res_o, load.at[4])
    out_r.start()

    for m in msg_d:
        m.wait_recv()
    y_strips(zx2, zy)

    def put_sen(x, v):
        sen[x] = v * CUBE

    def last(g, carry):
        yz_group(grid, zy, band, edge, g * 4, put_sen)
        return carry

    lax.fori_loop(0, 8, last, 0)
    out_s = pltpu.make_async_copy(sen, sen_o, load.at[5])
    out_s.start()
    for m in msg_a + msg_e + msg_b + msg_f + msg_d:
        m.wait_send()
    out_r.wait()
    out_s.wait()


def body(density, voxel_kind, velocity, adjoint):
    f32 = jnp.float32
    block = (X, Y, Z)
    strips, wide = (2, 2, Y, 128), (2, 2, 48, 128)
    return pl.pallas_call(
        kernel,
        out_shape=(jax.ShapeDtypeStruct((4, *block), f32), jax.ShapeDtypeStruct(block, f32)),
        in_specs=[pl.BlockSpec(memory_space=pl.ANY)] * 4,
        out_specs=(pl.BlockSpec(memory_space=pl.ANY),) * 2,
        scratch_shapes=[
            pltpu.VMEM((X, 48, Z), f32),
            pltpu.VMEM(block, jnp.int32),
            pltpu.VMEM((3, *block), f32),
            pltpu.VMEM((4, *block), f32),
            pltpu.VMEM(strips, f32),
            pltpu.VMEM(wide, f32),
            pltpu.VMEM(strips, f32),
            pltpu.VMEM(strips, f32),
            pltpu.VMEM(wide, f32),
            pltpu.VMEM((56, Y, Z), f32),
            pltpu.VMEM((44, Y, Z), f32),
            pltpu.VMEM((44, Y, Z), f32),
            pltpu.VMEM(block, f32),
            pltpu.VMEM((X, 48, Z), f32),
            pltpu.VMEM((4, *block), f32),
            pltpu.VMEM(block, f32),
            pltpu.VMEM((2, 4, Y, Z), f32),
            pltpu.VMEM((2, 4, Y, Z), f32),
            pltpu.VMEM((2, 4, X, 8, Z), f32),
            pltpu.VMEM((2, 4, X, 8, Z), f32),
            pltpu.VMEM((2, Y, 128), f32),
            pltpu.VMEM((2, Y, 128), f32),
            pltpu.VMEM((Z, Z), jnp.bfloat16),
            pltpu.VMEM((128, Z), jnp.bfloat16),
            pltpu.SemaphoreType.DMA((len(NAMES),)),
            pltpu.SemaphoreType.DMA((len(NAMES),)),
            pltpu.SemaphoreType.DMA((6,)),
        ],
        compiler_params=pltpu.CompilerParams(
            collective_id=0, has_side_effects=True, vmem_limit_bytes=44 * 2**20
        ),
    )(density, voxel_kind, velocity, adjoint)


def solution(mesh):
    own = P("gx", "gy", "gz")
    fields = P(None, "gx", "gy", "gz")
    return jax.shard_map(
        body, mesh=mesh, in_specs=(own, own, fields, fields), out_specs=(fields, own), check_vma=False
    )
```

```python
import math

import jax
import jax.numpy as jnp
from jax import lax
from jax.experimental import pallas as pl
from jax.experimental.pallas import tpu as pltpu
from jax.sharding import PartitionSpec as P

MESH = pl.DeviceIdType.MESH
NB = {"gx": 8, "gy": 4, "gz": 8}
X, Y, Z = 32, 32, 256
TANH2 = math.tanh(2.0)
CUBE = 1.0 / (49.0**3)

NAMES = (
    [f"a{c}{i}" for c in "yz" for i in (0, 1)]
    + [f"ad{i}{j}" for i in (0, 1) for j in (0, 1)]
    + [f"{c}{i}" for c in ("e", "bn", "bf", "fx", "fy", "fz", "dy", "dz") for i in (0, 1)]
    + [f"dd{i}{j}" for i in (0, 1) for j in (0, 1)]
)
SLOT = {n: i for i, n in enumerate(NAMES)}


def exists(offs):
    ok = None
    for axis, d in offs.items():
        i = lax.axis_index(axis)
        c = (i > 0) if d < 0 else (i < NB[axis] - 1)
        ok = c if ok is None else jnp.logical_and(ok, c)
    return ok


class Msg:
    def __init__(self, sems, name, offs, src, dst):
        self.offs = offs
        self.back = {a: -d for a, d in offs.items()}
        k = SLOT[name]
        self.copy = pltpu.make_async_remote_copy(
            src_ref=src,
            dst_ref=dst,
            send_sem=sems[0].at[k],
            recv_sem=sems[1].at[k],
            device_id={a: lax.axis_index(a) + d for a, d in offs.items()},
            device_id_type=MESH,
        )

    def start(self):
        @pl.when(exists(self.offs))
        def _():
            self.copy.start()

    def wait_recv(self):
        @pl.when(exists(self.back))
        def _():
            self.copy.wait_recv()

    def wait_send(self):
        @pl.when(exists(self.offs))
        def _():
            self.copy.wait_send()


def enter():
    barrier = pltpu.get_barrier_semaphore()
    total = jnp.int32(0)
    offs = [{a: d} for a in NB for d in (-1, 1)]
    offs += [{"gy": i, "gz": j} for i in (-1, 1) for j in (-1, 1)]
    for o in offs:
        c = exists(o)

        @pl.when(c)
        def _():
            pl.semaphore_signal(
                barrier, inc=1, device_id={a: lax.axis_index(a) + d for a, d in o.items()}, device_id_type=MESH
            )

        total = total + c.astype(jnp.int32)
    return barrier, total


def lanes(shape):
    return lax.broadcasted_iota(jnp.int32, shape, len(shape) - 1)


def rows(shape):
    return lax.broadcasted_iota(jnp.int32, shape, len(shape) - 2)


def y_filter(ref, *at):
    acc = 7.0 * ref[(*at, pl.ds(8, Y))]
    for k in range(1, 7):
        acc = acc + (7.0 - k) * (ref[(*at, pl.ds(8 - k, Y))] + ref[(*at, pl.ds(8 + k, Y))])
    return acc


def x_filter(ref, at):
    acc = 7.0 * ref[at + 6]
    for k in range(1, 7):
        acc = acc + (7.0 - k) * (ref[at + 6 - k] + ref[at + 6 + k])
    return acc


def split(v):
    hi = v.astype(jnp.bfloat16)
    lo = (v - hi.astype(jnp.float32)).astype(jnp.bfloat16)
    return jnp.concatenate([hi, lo], axis=0)


def pack_z(ref, first, out):
    slot = lanes((Y, 128)) // 8

    def pair(j, carry):
        left = jnp.zeros((Y, 128), jnp.float32)
        right = jnp.zeros((Y, 128), jnp.float32)
        for s in range(16):
            x = j * 16 + s
            a = ref[x, pl.ds(first, Y), 0:128]
            b = ref[x, pl.ds(first, Y), 128:256]
            a = a if s == 0 else pltpu.roll(a, 8 * s, 1)
            b = b if s == 15 else pltpu.roll(b, 8 * s + 8, 1)
            left = jnp.where(slot == s, a, left)
            right = jnp.where(slot == s, b, right)
        out[0, j] = left
        out[1, j] = right
        return carry

    lax.fori_loop(0, 2, pair, 0)


def y_strips(zx, zy):
    for side in (0, 1):
        for j in (0, 1):
            zy[side, j] = y_filter(zx, side, j)


def yz_group(ref, zy, band, edge, x0, put):
    lane = lanes((Y, 128))
    body = [y_filter(ref, x0 + i) for i in range(4)]
    ends = []
    for i in range(4):
        x = x0 + i
        s, j = x % 16, x // 16
        before = pltpu.roll(zy[0, j], 120 - 8 * s, 1)
        after = pltpu.roll(zy[1, j], 128 - 8 * s, 1)
        ends.append(jnp.where(lane < 64, after, before))
    full = split(jnp.concatenate(body, axis=0))
    tips = split(jnp.concatenate(ends, axis=0))
    res = jnp.dot(full, band[...], preferred_element_type=jnp.float32)
    res = res + jnp.dot(tips, edge[...], preferred_element_type=jnp.float32)
    res = res[: 4 * Y] + res[4 * Y :]
    for i in range(4):
        put(x0 + i, res[i * Y : (i + 1) * Y])


def y_up(v):
    return jnp.where(rows(v.shape) == Y - 1, 0.0, pltpu.roll(v, Y - 1, 0))


def y_dn(v):
    return jnp.where(rows(v.shape) == 0, 0.0, pltpu.roll(v, 1, 0))


def z_up(v):
    return jnp.where(lanes(v.shape) == Z - 1, 0.0, pltpu.roll(v, Z - 1, 1))


def z_dn(v):
    return jnp.where(lanes(v.shape) == 0, 0.0, pltpu.roll(v, 1, 1))


def kernel(
    den_h, kind_h, vel_h, adj_h, res, grid, zx2, band, edge,
    den, kind, vel, adj, zp, zx, zy, zp2, filt, em, pw, alpha,
    cxs, cxr, cys, cyr, czs, czr, send, recv, load,
):
    sems = (send, recv)
    ix, iy, iz = (lax.axis_index(a) for a in NB)
    loads = [
        pltpu.make_async_copy(den_h, den.at[:, pl.ds(8, Y), :], load.at[0]),
        pltpu.make_async_copy(vel_h, vel, load.at[1]),
        pltpu.make_async_copy(adj_h, adj, load.at[2]),
        pltpu.make_async_copy(kind_h, kind, load.at[3]),
    ]
    for c in loads:
        c.start()
    barrier, total = enter()

    @pl.when(ix == 0)
    def _():
        filt[0:12] = jnp.zeros((12, Y, Z), jnp.float32)
        em[0:6] = jnp.zeros((6, Y, Z), jnp.float32)
        cxr[0] = jnp.zeros((4, Y, Z), jnp.float32)

    @pl.when(ix == NB["gx"] - 1)
    def _():
        filt[44:56] = jnp.zeros((12, Y, Z), jnp.float32)
        em[38:44] = jnp.zeros((6, Y, Z), jnp.float32)
        cxr[1] = jnp.zeros((4, Y, Z), jnp.float32)

    @pl.when(iz == 0)
    def _():
        zx[0] = jnp.zeros((2, 48, 128), jnp.float32)
        zx2[0] = jnp.zeros((2, 48, 128), jnp.float32)
        czr[0] = jnp.zeros((Y, 128), jnp.float32)

    @pl.when(iz == NB["gz"] - 1)
    def _():
        zx[1] = jnp.zeros((2, 48, 128), jnp.float32)
        zx2[1] = jnp.zeros((2, 48, 128), jnp.float32)
        czr[1] = jnp.zeros((Y, 128), jnp.float32)

    for edge_at, first in ((0, 0), (NB["gy"] - 1, 40)):

        @pl.when(iy == edge_at)
        def _():
            for r in (zx, zx2):
                r[:, :, pl.ds(first, 8), :] = jnp.zeros((2, 2, 8, 128), jnp.float32)
            for r in (den, grid):
                r[:, pl.ds(first, 8), :] = jnp.zeros((X, 8, Z), jnp.float32)

    def clear(x, carry):
        for side in (0, 1):
            for c in range(4):
                cyr[side, c, x] = jnp.zeros((8, Z), jnp.float32)
        return carry

    lax.fori_loop(0, X, clear, 0)

    i, j = rows((Z, Z)), lanes((Z, Z))
    band[...] = jnp.maximum(7 - jnp.abs(i - j), 0).astype(jnp.float32).astype(jnp.bfloat16)
    i, j = rows((128, Z)), lanes((128, Z))
    i = jnp.where(i < 64, i + Z, i - 128)
    edge[...] = jnp.maximum(7 - jnp.abs(i - j), 0).astype(jnp.float32).astype(jnp.bfloat16)

    loads[0].wait()
    pack_z(den, 8, zp)
    pl.semaphore_wait(barrier, total)

    def yz_messages(name, src, packed, dst, strips, first):
        out = [
            Msg(sems, f"{name}y0", {"gy": -1}, src.at[:, pl.ds(first, 6), :], dst.at[:, pl.ds(40, 6), :]),
            Msg(sems, f"{name}y1", {"gy": 1}, src.at[:, pl.ds(first + 26, 6), :], dst.at[:, pl.ds(2, 6), :]),
            Msg(sems, f"{name}z0", {"gz": -1}, packed.at[0], strips.at[1, :, pl.ds(8, Y), :]),
            Msg(sems, f"{name}z1", {"gz": 1}, packed.at[1], strips.at[0, :, pl.ds(8, Y), :]),
        ]
        for a, (d, mine, there) in enumerate(((-1, 0, 40), (1, 26, 2))):
            for b, e in enumerate((-1, 1)):
                out.append(
                    Msg(
                        sems, f"{name}d{a}{b}", {"gy": d, "gz": e},
                        packed.at[b, :, pl.ds(mine, 6), :], strips.at[1 - b, :, pl.ds(there, 6), :],
                    )
                )
        return out

    msg_a = yz_messages("a", den, zp, den, zx, 8)
    for m in msg_a:
        m.start()

    for c in loads[1:]:
        c.wait()

    def energy(x, carry):
        e = None
        for d in range(3):
            u = vel[d, x]
            t = u * (u + adj[d, x])
            e = t if e is None else e + t
        em[x + 6] = jnp.where(kind[x] == 0, e, 0.0)
        return carry

    lax.fori_loop(0, X, energy, 0)
    msg_e = [
        Msg(sems, "e0", {"gx": -1}, em.at[6:12], em.at[38:44]),
        Msg(sems, "e1", {"gx": 1}, em.at[32:38], em.at[0:6]),
    ]
    for m in msg_e:
        m.start()

    lane = lanes((Y, 128))

    def stencil(x, carry, lower, upper):
        to_prev, to_next = carry
        lam = [adj[d, x] for d in range(3)]
        mu2 = adj[3, x] * 0.5
        w = [lam[d] + 2.0 * vel[d, x] for d in range(3)]
        plus = [w[d] + mu2 for d in range(3)]
        minus = [w[d] - mu2 for d in range(3)]

        def at(d, q):
            return adj[d, q] + 2.0 * vel[d, q]

        out = []
        for d in range(3):
            t = y_up(plus[1] if d == 1 else w[d]) + y_dn(minus[1] if d == 1 else w[d])
            t = t + z_up(plus[2] if d == 2 else w[d]) + z_dn(minus[2] if d == 2 else w[d])
            if lower:
                t = t + at(d, x - 1)
                if d == 0:
                    t = t - 0.5 * adj[3, x - 1]
            if upper:
                t = t + at(d, x + 1)
                if d == 0:
                    t = t + 0.5 * adj[3, x + 1]
            out.append(-t)
        div = y_up(lam[1]) - y_dn(lam[1]) + z_up(lam[2]) - z_dn(lam[2])
        if upper:
            div = div + adj[0, x + 1]
        if lower:
            div = div - adj[0, x - 1]
        out.append(-0.5 * div)
        for c in range(4):
            res[c, x] = out[c]

        if not lower:
            cxs[0, 0], cxs[0, 1], cxs[0, 2], cxs[0, 3] = -plus[0], -w[1], -w[2], -0.5 * lam[0]
        if not upper:
            cxs[1, 0], cxs[1, 1], cxs[1, 2], cxs[1, 3] = -minus[0], -w[1], -w[2], 0.5 * lam[0]
        for side, part, end, sign in ((0, plus, slice(0, 8), -0.5), (1, minus, slice(Y - 8, Y), 0.5)):
            cys[side, 0, x] = -w[0][end]
            cys[side, 1, x] = -part[1][end]
            cys[side, 2, x] = -w[2][end]
            cys[side, 3, x] = sign * lam[1][end]
        zs0 = (-w[0], -w[1], -plus[2], -0.5 * lam[2])
        zs1 = (-w[0], -w[1], -minus[2], 0.5 * lam[2])
        for c in range(4):
            at_lane = c * X + x
            first = pltpu.roll(zs0[c][:, 0:128], at_lane, 1)
            last = pltpu.roll(zs1[c][:, 128:256], lax.rem(at_lane + 1, 128), 1)
            to_prev = jnp.where(lane == at_lane, first, to_prev)
            to_next = jnp.where(lane == at_lane, last, to_next)
        return to_prev, to_next

    ends = (jnp.zeros((Y, 128), jnp.float32), jnp.zeros((Y, 128), jnp.float32))
    ends = stencil(0, ends, False, True)
    ends = lax.fori_loop(1, X - 1, lambda x, c: stencil(x, c, True, True), ends)
    ends = stencil(X - 1, ends, True, False)
    czs[0], czs[1] = ends

    msg_f = [
        Msg(sems, "fx0", {"gx": -1}, cxs.at[0], cxr.at[1]),
        Msg(sems, "fx1", {"gx": 1}, cxs.at[1], cxr.at[0]),
        Msg(sems, "fy0", {"gy": -1}, cys.at[0, :, :, 0:1, :], cyr.at[1, :, :, 7:8, :]),
        Msg(sems, "fy1", {"gy": 1}, cys.at[1, :, :, 7:8, :], cyr.at[0, :, :, 0:1, :]),
        Msg(sems, "fz0", {"gz": -1}, czs.at[0], czr.at[1]),
        Msg(sems, "fz1", {"gz": 1}, czs.at[1], czr.at[0]),
    ]

    for m in msg_a:
        m.wait_recv()
    y_strips(zx, zy)

    def put_filt(x, v):
        filt[x + 12] = v

    def outer(g, carry):
        yz_group(den, zy, band, edge, g * 4, put_filt)
        yz_group(den, zy, band, edge, 20 + g * 4, put_filt)
        return carry

    lax.fori_loop(0, 3, outer, 0)
    msg_b = [
        Msg(sems, "bn0", {"gx": -1}, filt.at[12:18], filt.at[44:50]),
        Msg(sems, "bn1", {"gx": 1}, filt.at[38:44], filt.at[6:12]),
        Msg(sems, "bf0", {"gx": -1}, filt.at[18:24], filt.at[50:56]),
        Msg(sems, "bf1", {"gx": 1}, filt.at[32:38], filt.at[0:6]),
    ]
    for m in msg_b:
        m.start()
    for m in msg_f:
        m.start()
    for g in (12, 16):
        yz_group(den, zy, band, edge, g, put_filt)

    def project(e):
        t = jnp.tanh(x_filter(filt, e) * (4.0 * CUBE) - 2.0)
        r = 1.0 / (1.0 + (TANH2 + t) * (0.5 / TANH2))
        pw[e] = (-8.0 / TANH2) * (r * r) * (1.0 - t * t) * em[e]
        return r

    def project_own(x, carry):
        r = project(x + 6)
        k = kind[x]
        alpha[x] = jnp.where(k == 0, 4.0 * r - 2.0, jnp.where(k == 1, 2.0, 0.0))
        return carry

    def project_halo(e, carry):
        project(e)
        return carry

    def smooth_x(x, carry):
        grid[x, pl.ds(8, Y), :] = x_filter(pw, x)
        return carry

    lax.fori_loop(6, 26, project_own, 0)
    for m in msg_b[:2]:
        m.wait_recv()
    for lo, hi in ((0, 6), (26, 32)):
        lax.fori_loop(lo, hi, project_own, 0)
    lax.fori_loop(6, 26, smooth_x, 0)
    for m in msg_e:
        m.wait_recv()
    for m in msg_b[2:]:
        m.wait_recv()
    for lo, hi in ((0, 6), (38, 44)):
        lax.fori_loop(lo, hi, project_halo, 0)
    for lo, hi in ((0, 6), (26, 32)):
        lax.fori_loop(lo, hi, smooth_x, 0)

    pack_z(grid, 8, zp2)
    msg_d = yz_messages("d", grid, zp2, grid, zx2, 8)
    for m in msg_d:
        m.start()

    for m in msg_f:
        m.wait_recv()
    for c in range(4):
        res[c, 0] += cxr[0, c]
        res[c, X - 1] += cxr[1, c]

    def finish(x, carry):
        a = alpha[x] + 6.0
        k = kind[x]
        for c in range(4):
            at_lane = c * X + x
            first = pltpu.roll(czr[0], lax.rem(128 - at_lane, 128), 1)
            last = pltpu.roll(czr[1], 127 - at_lane, 1)
            res[c, x, 0:8] += cyr[0, c, x]
            res[c, x, Y - 8 : Y] += cyr[1, c, x]
            r = res[c, x] + jnp.concatenate([jnp.where(lane == 0, first, 0.0), jnp.where(lane == 127, last, 0.0)], axis=1)
            v = adj[c, x]
            if c < 3:
                res[c, x] = jnp.where(k == 2, v, r + a * (v + 2.0 * vel[c, x]))
            else:
                res[c, x] = jnp.where(k == 3, v, r)
        return carry

    lax.fori_loop(0, X, finish, 0)

    for m in msg_d:
        m.wait_recv()
    for m in msg_a + msg_e + msg_b + msg_f + msg_d:
        m.wait_send()


def finish_kernel(res, grid, zx2, band, edge, res_o, sen_o, zy, sen, sems):
    out_r = pltpu.make_async_copy(res, res_o, sems.at[0])
    out_r.start()
    y_strips(zx2, zy)

    def put_sen(x, v):
        sen[x] = v * CUBE

    def last(g, carry):
        yz_group(grid, zy, band, edge, g * 4, put_sen)
        return carry

    lax.fori_loop(0, 8, last, 0)
    out_s = pltpu.make_async_copy(sen, sen_o, sems.at[1])
    out_s.start()
    out_r.wait()
    out_s.wait()


def body(*args):
    f32 = jnp.float32
    block = (X, Y, Z)
    strips, wide = (2, 2, Y, 128), (2, 2, 48, 128)
    vmem = pl.BlockSpec(memory_space=pltpu.VMEM)
    near = pl.pallas_call(
        kernel,
        out_shape=(
            pltpu.VMEM((4, *block), f32),
            pltpu.VMEM((X, 48, Z), f32),
            pltpu.VMEM(wide, f32),
            pltpu.VMEM((Z, Z), jnp.bfloat16),
            pltpu.VMEM((128, Z), jnp.bfloat16),
        ),
        in_specs=[pl.BlockSpec(memory_space=pl.ANY)] * 4,
        out_specs=(vmem,) * 5,
        scratch_shapes=[
            pltpu.VMEM((X, 48, Z), f32),
            pltpu.VMEM(block, jnp.int32),
            pltpu.VMEM((3, *block), f32),
            pltpu.VMEM((4, *block), f32),
            pltpu.VMEM(strips, f32),
            pltpu.VMEM(wide, f32),
            pltpu.VMEM(strips, f32),
            pltpu.VMEM(strips, f32),
            pltpu.VMEM((56, Y, Z), f32),
            pltpu.VMEM((44, Y, Z), f32),
            pltpu.VMEM((44, Y, Z), f32),
            pltpu.VMEM(block, f32),
            pltpu.VMEM((2, 4, Y, Z), f32),
            pltpu.VMEM((2, 4, Y, Z), f32),
            pltpu.VMEM((2, 4, X, 8, Z), f32),
            pltpu.VMEM((2, 4, X, 8, Z), f32),
            pltpu.VMEM((2, Y, 128), f32),
            pltpu.VMEM((2, Y, 128), f32),
            pltpu.SemaphoreType.DMA((len(NAMES),)),
            pltpu.SemaphoreType.DMA((len(NAMES),)),
            pltpu.SemaphoreType.DMA((4,)),
        ],
        compiler_params=pltpu.CompilerParams(
            collective_id=0, has_side_effects=True, vmem_limit_bytes=32 * 2**20
        ),
    )(*(pltpu.with_memory_space_constraint(a, pltpu.HBM) for a in args))
    return pl.pallas_call(
        finish_kernel,
        out_shape=(jax.ShapeDtypeStruct((4, *block), f32), jax.ShapeDtypeStruct(block, f32)),
        in_specs=[vmem] * 5,
        out_specs=(pl.BlockSpec(memory_space=pl.ANY),) * 2,
        scratch_shapes=[
            pltpu.VMEM(strips, f32),
            pltpu.VMEM(block, f32),
            pltpu.SemaphoreType.DMA((2,)),
        ],
        compiler_params=pltpu.CompilerParams(vmem_limit_bytes=16 * 2**20),
    )(*near)


def solution(mesh):
    own = P("gx", "gy", "gz")
    fields = P(None, "gx", "gy", "gz")
    return jax.shard_map(
        body, mesh=mesh, in_specs=(own, own, fields, fields), out_specs=(fields, own), check_vma=False
    )
```

```python
import math

import jax
import jax.numpy as jnp
from jax import lax
from jax.experimental import pallas as pl
from jax.experimental.pallas import tpu as pltpu
from jax.sharding import PartitionSpec as P

MESH = pl.DeviceIdType.MESH
NB = {"gx": 8, "gy": 4, "gz": 8}
X, Y, Z = 32, 32, 256
TANH2 = math.tanh(2.0)
CUBE = 1.0 / (49.0**3)

NAMES = (
    [f"{k}y{i}{part}" for k in "ad" for i in (0, 1) for part in "lhm"]
    + [f"{k}z{i}" for k in "ad" for i in (0, 1)]
    + [f"{k}d{i}{j}" for k in "ad" for i in (0, 1) for j in (0, 1)]
    + [f"{c}{k}{i}" for c in "bc" for k in range(3) for i in (0, 1)]
    + [f"f{c}{i}" for c in "xyz" for i in (0, 1)]
)
PARTS = {"l": (0, 6), "h": (26, 32), "m": (6, 26)}
SLOT = {n: i for i, n in enumerate(NAMES)}


def exists(offs):
    ok = None
    for axis, d in offs.items():
        i = lax.axis_index(axis)
        c = (i > 0) if d < 0 else (i < NB[axis] - 1)
        ok = c if ok is None else jnp.logical_and(ok, c)
    return ok


class Msg:
    def __init__(self, sems, name, offs, src, dst):
        self.offs = offs
        self.back = {a: -d for a, d in offs.items()}
        k = SLOT[name]
        self.copy = pltpu.make_async_remote_copy(
            src_ref=src,
            dst_ref=dst,
            send_sem=sems[0].at[k],
            recv_sem=sems[1].at[k],
            device_id={a: lax.axis_index(a) + d for a, d in offs.items()},
            device_id_type=MESH,
        )

    def start(self):
        @pl.when(exists(self.offs))
        def _():
            self.copy.start()

    def wait_recv(self):
        @pl.when(exists(self.back))
        def _():
            self.copy.wait_recv()

    def wait_send(self):
        @pl.when(exists(self.offs))
        def _():
            self.copy.wait_send()


def enter():
    barrier = pltpu.get_barrier_semaphore()
    total = jnp.int32(0)
    offs = [{a: d} for a in NB for d in (-1, 1)]
    offs += [{"gy": i, "gz": j} for i in (-1, 1) for j in (-1, 1)]
    for o in offs:
        c = exists(o)

        @pl.when(c)
        def _():
            pl.semaphore_signal(
                barrier, inc=1, device_id={a: lax.axis_index(a) + d for a, d in o.items()}, device_id_type=MESH
            )

        total = total + c.astype(jnp.int32)
    return barrier, total


def lanes(shape):
    return lax.broadcasted_iota(jnp.int32, shape, len(shape) - 1)


def rows(shape):
    return lax.broadcasted_iota(jnp.int32, shape, len(shape) - 2)


def y_filter(ref, *at):
    acc = 7.0 * ref[(*at, pl.ds(8, Y))]
    for k in range(1, 7):
        acc = acc + (7.0 - k) * (ref[(*at, pl.ds(8 - k, Y))] + ref[(*at, pl.ds(8 + k, Y))])
    return acc


def y_local(v):
    def run(u):
        n = u.shape[0]
        two = u[: n - 1] + u[1:]
        three = two[: n - 2] + u[2:]
        four = three[: n - 3] + u[3:]
        return four[: n - 6] + three[4 : n - 2]

    zero = jnp.zeros((8, Z), jnp.float32)
    return run(run(jnp.concatenate([zero, v, zero], axis=0)[2:46]))


def x_run(ref, e, n, at):
    v = [ref[e + i, pl.ds(at, 8), :] for i in range(n + 12)]
    for _ in range(2):
        t = v[0]
        for u in v[1:7]:
            t = t + u
        out = [t]
        for i in range(7, len(v)):
            t = t + (v[i] - v[i - 7])
            out.append(t)
        v = out
    return v


def split(v):
    hi = v.astype(jnp.bfloat16)
    lo = (v - hi.astype(jnp.float32)).astype(jnp.bfloat16)
    return jnp.concatenate([hi, lo], axis=0)


def times(v, mat):
    n = v.shape[0]
    r = jnp.dot(split(v), mat[...], preferred_element_type=jnp.float32)
    return r[:n] + r[n:]


def fill_mats(band, tips):
    def put(ref, dist):
        ref[...] = jnp.maximum(7 - dist, 0).astype(jnp.float32).astype(jnp.bfloat16)

    i, j = rows((Z, Z)), lanes((Z, Z))
    put(band, jnp.abs(i - j))
    i, j = rows((128, 128)), lanes((128, 128))
    same = i // 8 == j // 8
    put(tips.at[0], jnp.where(same, 8 + j - i, 9))
    put(tips.at[1], jnp.where(same, 8 + i - j, 9))


def pack_z(ref, xs, out, fresh):
    slot = lanes((Y, 128)) // 8
    for j in (0, 1):
        left = jnp.zeros((Y, 128), jnp.float32) if fresh else out[0, j]
        right = jnp.zeros((Y, 128), jnp.float32) if fresh else out[1, j]
        for x in xs:
            if x // 16 != j:
                continue
            s = x % 16
            a = ref[x, :, 0:128]
            b = ref[x, :, 128:256]
            a = a if s == 0 else pltpu.roll(a, 8 * s, 1)
            b = b if s == 15 else pltpu.roll(b, 8 * s + 8, 1)
            left = jnp.where(slot == s, a, left)
            right = jnp.where(slot == s, b, right)
        out[0, j] = left
        out[1, j] = right


def yz_local(ref, band, x0, n, put):
    v = times(jnp.concatenate([y_local(ref[x0 + i]) for i in range(n)], axis=0), band)
    for i in range(n):
        put(x0 + i, v[i * Y : (i + 1) * Y])


def z_strips(strips, tips, zy):
    for side in (0, 1):
        v = jnp.concatenate([y_filter(strips, side, j) for j in (0, 1)], axis=0)
        v = times(v, tips.at[side])
        for j in (0, 1):
            zy[side, j] = v[j * Y : (j + 1) * Y]


def y_faces(faces, band, x0, n):
    out = []
    row = rows((n, 8, Z))
    for side in (0, 1):
        t = faces[side, x0 : x0 + n]
        acc = None
        for k in range(1, 7):
            if side == 0:
                u = jnp.where(row < k, (7.0 - k) * pltpu.roll(t, k, 1), 0.0)
            else:
                u = jnp.where(row >= 8 - k, (7.0 - k) * pltpu.roll(t, 8 - k, 1), 0.0)
            acc = u if acc is None else acc + u
        out.append(acc.reshape(n * 8, Z))
    v = times(jnp.concatenate(out, axis=0), band)
    return v[: n * 8].reshape(n, 8, Z), v[n * 8 :].reshape(n, 8, Z)


def yz_halo(faces, zy, band, x0, n, old, put):
    lane = lanes((Y, 128))
    first, last = y_faces(faces, band, x0, n)
    for i in range(n):
        x = x0 + i
        s, j = x % 16, x // 16
        lo, hi = zy[0, j], zy[1, j]
        lo = lo if s == 0 else pltpu.roll(lo, 128 - 8 * s, 1)
        hi = hi if s == 15 else pltpu.roll(hi, 120 - 8 * s, 1)
        v = old(x) + jnp.concatenate([jnp.where(lane < 8, lo, 0.0), jnp.where(lane >= 120, hi, 0.0)], axis=1)
        put(x, jnp.concatenate([v[0:8] + first[i], v[8 : Y - 8], v[Y - 8 : Y] + last[i]], axis=0))


def y_up(v):
    return jnp.where(rows(v.shape) == Y - 1, 0.0, pltpu.roll(v, Y - 1, 0))


def y_dn(v):
    return jnp.where(rows(v.shape) == 0, 0.0, pltpu.roll(v, 1, 0))


def z_up(v):
    return jnp.where(lanes(v.shape) == Z - 1, 0.0, pltpu.roll(v, Z - 1, 1))


def z_dn(v):
    return jnp.where(lanes(v.shape) == 0, 0.0, pltpu.roll(v, 1, 1))


def kernel(
    den_h, kind_h, vel_h, adj_h, res, sen, yf2, zx2, band, tips,
    den, kind, vel, adj, zp, yf, zx, zy, zp2, filt, em, pw, alpha, grid,
    cxs, cxr, cys, cyr, czs, czr, send, recv, load,
):
    sems = (send, recv)
    ix, iy, iz = (lax.axis_index(a) for a in NB)
    loads = [
        pltpu.make_async_copy(den_h, den, load.at[0]),
        pltpu.make_async_copy(vel_h, vel, load.at[1]),
        pltpu.make_async_copy(adj_h, adj, load.at[2]),
        pltpu.make_async_copy(kind_h, kind, load.at[3]),
    ]
    for c in loads:
        c.start()
    barrier, total = enter()

    f32 = jnp.float32

    @pl.when(ix == 0)
    def _():
        filt[0:6] = jnp.zeros((6, Y, Z), f32)
        pw[0:6] = jnp.zeros((6, Y, Z), f32)
        cxr[0] = jnp.zeros((4, Y, Z), f32)

    @pl.when(ix == NB["gx"] - 1)
    def _():
        filt[38:44] = jnp.zeros((6, Y, Z), f32)
        pw[38:44] = jnp.zeros((6, Y, Z), f32)
        cxr[1] = jnp.zeros((4, Y, Z), f32)

    for side, at in ((0, 0), (1, NB["gz"] - 1)):

        @pl.when(iz == at)
        def _():
            zx[side] = jnp.zeros((2, 48, 128), f32)
            zx2[side] = jnp.zeros((2, 48, 128), f32)
            czr[side] = jnp.zeros((Y, 128), f32)

    for side, at in ((0, 0), (1, NB["gy"] - 1)):

        @pl.when(iy == at)
        def _():
            for r in (zx, zx2):
                r[:, :, pl.ds(40 * side, 8), :] = jnp.zeros((2, 2, 8, 128), f32)
            for r in (yf, yf2):
                r[side] = jnp.zeros((X, 8, Z), f32)
            cyr[side] = jnp.zeros((4, X, Z), f32)

    fill_mats(band, tips)

    def face_messages(name, src, faces, parts):
        out = []
        for p in parts:
            lo, hi = PARTS[p]
            xs = pl.ds(lo, hi - lo)
            out += [
                Msg(sems, f"{name}y0{p}", {"gy": -1}, src.at[xs, 0:6, :], faces.at[1, xs, 0:6, :]),
                Msg(sems, f"{name}y1{p}", {"gy": 1}, src.at[xs, Y - 6 : Y, :], faces.at[0, xs, 2:8, :]),
            ]
        return out

    def strip_messages(name, packed, strips):
        out = [
            Msg(sems, f"{name}z0", {"gz": -1}, packed.at[0], strips.at[1, :, pl.ds(8, Y), :]),
            Msg(sems, f"{name}z1", {"gz": 1}, packed.at[1], strips.at[0, :, pl.ds(8, Y), :]),
        ]
        for a, (d, mine, there) in enumerate(((-1, 0, 40), (1, 26, 2))):
            for b, e in enumerate((-1, 1)):
                out.append(
                    Msg(
                        sems, f"{name}d{a}{b}", {"gy": d, "gz": e},
                        packed.at[b, :, pl.ds(mine, 6), :], strips.at[1 - b, :, pl.ds(there, 6), :],
                    )
                )
        return out

    loads[0].wait()
    pack_z(den, range(X), zp, True)
    pl.semaphore_wait(barrier, total)
    msg_an = face_messages("a", den, yf, "lh")
    msg_az = strip_messages("a", zp, zx)
    msg_am = face_messages("a", den, yf, "m")
    for m in msg_an + msg_az + msg_am:
        m.start()

    for c in loads[1:]:
        c.wait()

    for side, x, sign in ((0, 0, 0.5), (1, X - 1, -0.5)):
        w = [adj[d, x] + 2.0 * vel[d, x] for d in range(3)]
        cxs[side, 0] = -(w[0] + sign * adj[3, x])
        cxs[side, 1] = -w[1]
        cxs[side, 2] = -w[2]
        cxs[side, 3] = -sign * adj[0, x]
    msg_f = [
        Msg(sems, "fx0", {"gx": -1}, cxs.at[0], cxr.at[1]),
        Msg(sems, "fx1", {"gx": 1}, cxs.at[1], cxr.at[0]),
        Msg(sems, "fy0", {"gy": -1}, cys.at[0], cyr.at[1]),
        Msg(sems, "fy1", {"gy": 1}, cys.at[1], cyr.at[0]),
        Msg(sems, "fz0", {"gz": -1}, czs.at[0], czr.at[1]),
        Msg(sems, "fz1", {"gz": 1}, czs.at[1], czr.at[0]),
    ]

    for m in msg_f[:2]:
        m.start()

    def energy(x, carry):
        e = None
        for d in range(3):
            u = vel[d, x]
            t = u * (u + adj[d, x])
            e = t if e is None else e + t
        em[x] = jnp.where(kind[x] == 0, e, 0.0)
        return carry

    lax.fori_loop(0, X, energy, 0)

    def put_filt(x, v):
        filt[x + 6] = v

    def old_filt(x):
        return filt[x + 6]

    for x0, n in ((0, 6), (26, 6), (6, 10), (16, 10)):
        yz_local(den, band, x0, n, put_filt)

    lane = lanes((Y, 128))

    def stencil(x, carry, lower, upper):
        to_prev, to_next = carry
        lam = [adj[d, x] for d in range(3)]
        mu2 = adj[3, x] * 0.5
        w = [lam[d] + 2.0 * vel[d, x] for d in range(3)]
        plus = [w[d] + mu2 for d in range(3)]
        minus = [w[d] - mu2 for d in range(3)]

        def at(d, q):
            return adj[d, q] + 2.0 * vel[d, q]

        out = []
        for d in range(3):
            t = y_up(plus[1] if d == 1 else w[d]) + y_dn(minus[1] if d == 1 else w[d])
            t = t + z_up(plus[2] if d == 2 else w[d]) + z_dn(minus[2] if d == 2 else w[d])
            if lower:
                t = t + at(d, x - 1)
                if d == 0:
                    t = t - 0.5 * adj[3, x - 1]
            if upper:
                t = t + at(d, x + 1)
                if d == 0:
                    t = t + 0.5 * adj[3, x + 1]
            out.append(-t)
        div = y_up(lam[1]) - y_dn(lam[1]) + z_up(lam[2]) - z_dn(lam[2])
        if upper:
            div = div + adj[0, x + 1]
        if lower:
            div = div - adj[0, x - 1]
        out.append(-0.5 * div)
        for c in range(4):
            res[c, x] = out[c]

        for side, part, end, sign in ((0, plus, slice(0, 1), -0.5), (1, minus, slice(Y - 1, Y), 0.5)):
            cys[side, 0, pl.ds(x, 1)] = -w[0][end]
            cys[side, 1, pl.ds(x, 1)] = -part[1][end]
            cys[side, 2, pl.ds(x, 1)] = -w[2][end]
            cys[side, 3, pl.ds(x, 1)] = sign * lam[1][end]
        zs0 = (-w[0], -w[1], -plus[2], -0.5 * lam[2])
        zs1 = (-w[0], -w[1], -minus[2], 0.5 * lam[2])
        for c in range(4):
            at_lane = c * X + x
            first = pltpu.roll(zs0[c][:, 0:128], at_lane, 1)
            last = pltpu.roll(zs1[c][:, 128:256], lax.rem(at_lane + 1, 128), 1)
            to_prev = jnp.where(lane == at_lane, first, to_prev)
            to_next = jnp.where(lane == at_lane, last, to_next)
        return to_prev, to_next

    ends = (jnp.zeros((Y, 128), f32), jnp.zeros((Y, 128), f32))
    ends = stencil(0, ends, False, True)
    ends = lax.fori_loop(1, 12, lambda x, c: stencil(x, c, True, True), ends)

    for m in msg_an + msg_az:
        m.wait_recv()
    z_strips(zx, tips, zy)

    def x_messages(name, ref):
        out = []
        for k in range(3):
            out.append([
                Msg(sems, f"{name}{k}0", {"gx": -1}, ref.at[pl.ds(6 + 2 * k, 2)], ref.at[pl.ds(38 + 2 * k, 2)]),
                Msg(sems, f"{name}{k}1", {"gx": 1}, ref.at[pl.ds(36 - 2 * k, 2)], ref.at[pl.ds(4 - 2 * k, 2)]),
            ])
        return out

    msg_b = x_messages("b", filt)
    for x0 in (0, 26):
        yz_halo(yf, zy, band, x0, 6, old_filt, put_filt)
    for ms in msg_b:
        for m in ms:
            m.start()
    for m in msg_am:
        m.wait_recv()
    for x0 in (6, 16):
        yz_halo(yf, zy, band, x0, 10, old_filt, put_filt)

    def project(x, n):
        def strip(q, carry):
            at = pl.multiple_of(q * 8, 8)
            for i, f in enumerate(x_run(filt, x, n, at)):
                t = jnp.tanh(f * (4.0 * CUBE) - 2.0)
                r = 1.0 / (1.0 + (TANH2 + t) * (0.5 / TANH2))
                here = (x + i, pl.ds(at, 8))
                pw[x + i + 6, pl.ds(at, 8)] = (-8.0 / TANH2) * (r * r) * (1.0 - t * t) * em[here]
                k = kind[here]
                alpha[here] = jnp.where(k == 0, 4.0 * r - 2.0, jnp.where(k == 1, 2.0, 0.0))
            return carry

        lax.fori_loop(0, Y // 8, strip, 0)

    def smooth_x(x, n):
        def strip(q, carry):
            at = pl.multiple_of(q * 8, 8)
            for i, f in enumerate(x_run(pw, x, n, at)):
                grid[x + i, pl.ds(at, 8)] = f
            return carry

        lax.fori_loop(0, Y // 8, strip, 0)

    def put_sen(x, v):
        sen[x] = v

    for x in (6, 16):
        project(x, 10)

    ends = lax.fori_loop(12, X - 1, lambda x, c: stencil(x, c, True, True), ends)
    ends = stencil(X - 1, ends, True, False)
    czs[0], czs[1] = ends
    for m in msg_f[2:]:
        m.start()

    msg_c = x_messages("c", pw)
    for k in range(3):
        for m in msg_b[k]:
            m.wait_recv()
        for x in (4 - 2 * k, 26 + 2 * k):
            project(x, 2)
        for m in msg_c[2 - k]:
            m.start()

    for x in (6, 16):
        smooth_x(x, 10)
    msg_dm = face_messages("d", grid, yf2, "m")
    for m in msg_dm:
        m.start()
    pack_z(grid, range(6, 26), zp2, True)
    for x0 in (6, 16):
        yz_local(grid, band, x0, 10, put_sen)

    for m in msg_f[2:]:
        m.wait_recv()

    def finish(x, carry):
        a = alpha[x] + 6.0
        k = kind[x]
        row = rows((8, Z))
        for c in range(4):
            at_lane = c * X + x
            first = pltpu.roll(czr[0], (128 - at_lane) % 128, 1)
            last = pltpu.roll(czr[1], 127 - at_lane, 1)
            top = jnp.where(row == 0, cyr[0, c, pl.ds(x, 1)], 0.0)
            end = jnp.where(row == 7, cyr[1, c, pl.ds(x, 1)], 0.0)
            r = res[c, x]
            r = jnp.concatenate([r[0:8] + top, r[8 : Y - 8], r[Y - 8 : Y] + end], axis=0)
            r = r + jnp.concatenate([jnp.where(lane == 0, first, 0.0), jnp.where(lane == 127, last, 0.0)], axis=1)
            v = adj[c, x]
            if c < 3:
                res[c, x] = jnp.where(k == 2, v, r + a * (v + 2.0 * vel[c, x]))
            else:
                res[c, x] = jnp.where(k == 3, v, r)
        return carry

    lax.fori_loop(1, 12, finish, 0)
    for ms in msg_c:
        for m in ms:
            m.wait_recv()
    for x in (0, 26):
        smooth_x(x, 6)

    msg_dn = face_messages("d", grid, yf2, "lh")
    for m in msg_dn:
        m.start()
    pack_z(grid, (*range(0, 6), *range(26, 32)), zp2, False)
    msg_dz = strip_messages("d", zp2, zx2)
    for m in msg_dz:
        m.start()
    for x0 in (0, 26):
        yz_local(grid, band, x0, 6, put_sen)

    lax.fori_loop(12, X - 1, finish, 0)
    for m in msg_f[:2]:
        m.wait_recv()
    for side, x in ((0, 0), (1, X - 1)):
        for c in range(4):
            res[c, x] += cxr[side, c]
        finish(x, 0)

    for m in msg_dn + msg_dm + msg_dz:
        m.wait_recv()
    for m in msg_an + msg_am + msg_az + sum(msg_b + msg_c, []) + msg_f + msg_dn + msg_dm + msg_dz:
        m.wait_send()


def finish_kernel(res, sen_in, yf2, zx2, band, tips, res_o, sen_o, zy, sen, sems):
    out_r = pltpu.make_async_copy(res, res_o, sems.at[0])
    out_r.start()
    z_strips(zx2, tips, zy)

    def old(x):
        return sen_in[x]

    def put(x, v):
        sen[x] = v * CUBE

    out_s = []
    for g in range(2):
        yz_halo(yf2, zy, band, g * 16, 16, old, put)
        part = pl.ds(g * 16, 16)
        out_s.append(pltpu.make_async_copy(sen.at[part], sen_o.at[part], sems.at[1 + g]))
        out_s[-1].start()
    out_r.wait()
    for c in out_s:
        c.wait()


def body(*args):
    f32 = jnp.float32
    block = (X, Y, Z)
    strips, wide = (2, 2, Y, 128), (2, 2, 48, 128)
    vmem = pl.BlockSpec(memory_space=pltpu.VMEM)
    near = pl.pallas_call(
        kernel,
        out_shape=(
            pltpu.VMEM((4, *block), f32),
            pltpu.VMEM(block, f32),
            pltpu.VMEM((2, X, 8, Z), f32),
            pltpu.VMEM(wide, f32),
            pltpu.VMEM((Z, Z), jnp.bfloat16),
            pltpu.VMEM((2, 128, 128), jnp.bfloat16),
        ),
        in_specs=[pl.BlockSpec(memory_space=pl.ANY)] * 4,
        out_specs=(vmem,) * 6,
        scratch_shapes=[
            pltpu.VMEM(block, f32),
            pltpu.VMEM(block, jnp.int32),
            pltpu.VMEM((3, *block), f32),
            pltpu.VMEM((4, *block), f32),
            pltpu.VMEM(strips, f32),
            pltpu.VMEM((2, X, 8, Z), f32),
            pltpu.VMEM(wide, f32),
            pltpu.VMEM(strips, f32),
            pltpu.VMEM(strips, f32),
            pltpu.VMEM((44, Y, Z), f32),
            pltpu.VMEM(block, f32),
            pltpu.VMEM((44, Y, Z), f32),
            pltpu.VMEM(block, f32),
            pltpu.VMEM(block, f32),
            pltpu.VMEM((2, 4, Y, Z), f32),
            pltpu.VMEM((2, 4, Y, Z), f32),
            pltpu.VMEM((2, 4, X, Z), f32),
            pltpu.VMEM((2, 4, X, Z), f32),
            pltpu.VMEM((2, Y, 128), f32),
            pltpu.VMEM((2, Y, 128), f32),
            pltpu.SemaphoreType.DMA((len(NAMES),)),
            pltpu.SemaphoreType.DMA((len(NAMES),)),
            pltpu.SemaphoreType.DMA((4,)),
        ],
        compiler_params=pltpu.CompilerParams(
            collective_id=0, has_side_effects=True, vmem_limit_bytes=32 * 2**20
        ),
    )(*(pltpu.with_memory_space_constraint(a, pltpu.HBM) for a in args))
    return pl.pallas_call(
        finish_kernel,
        out_shape=(jax.ShapeDtypeStruct((4, *block), f32), jax.ShapeDtypeStruct(block, f32)),
        in_specs=[vmem] * 6,
        out_specs=(pl.BlockSpec(memory_space=pl.ANY),) * 2,
        scratch_shapes=[
            pltpu.VMEM(strips, f32),
            pltpu.VMEM(block, f32),
            pltpu.SemaphoreType.DMA((3,)),
        ],
        compiler_params=pltpu.CompilerParams(vmem_limit_bytes=16 * 2**20),
    )(*near)


def solution(mesh):
    own = P("gx", "gy", "gz")
    fields = P(None, "gx", "gy", "gz")
    return jax.shard_map(
        body, mesh=mesh, in_specs=(own, own, fields, fields), out_specs=(fields, own), check_vma=False
    )
```

```python
import math

import jax
import jax.numpy as jnp
from jax import lax
from jax.experimental import pallas as pl
from jax.experimental.pallas import tpu as pltpu
from jax.sharding import PartitionSpec as P

MESH = pl.DeviceIdType.MESH
NB = {"gx": 8, "gy": 4, "gz": 8}
X, Y, Z = 32, 32, 256
TANH2 = math.tanh(2.0)
CUBE = 1.0 / (49.0**3)

NAMES = (
    [f"{k}y{i}{part}" for k in "ad" for i in (0, 1) for part in "lhm"]
    + [f"{k}z{i}" for k in "ad" for i in (0, 1)]
    + [f"{k}d{i}{j}" for k in "ad" for i in (0, 1) for j in (0, 1)]
    + [f"{c}{k}{i}" for c in "bc" for k in range(3) for i in (0, 1)]
    + [f"f{c}{i}" for c in "xyz" for i in (0, 1)]
)
PARTS = {"l": (0, 6), "h": (26, 32), "m": (6, 26)}
SLOT = {n: i for i, n in enumerate(NAMES)}


def exists(offs):
    ok = None
    for axis, d in offs.items():
        i = lax.axis_index(axis)
        c = (i > 0) if d < 0 else (i < NB[axis] - 1)
        ok = c if ok is None else jnp.logical_and(ok, c)
    return ok


class Msg:
    def __init__(self, sems, name, offs, src, dst):
        self.offs = offs
        self.back = {a: -d for a, d in offs.items()}
        k = SLOT[name]
        self.copy = pltpu.make_async_remote_copy(
            src_ref=src,
            dst_ref=dst,
            send_sem=sems[0].at[k],
            recv_sem=sems[1].at[k],
            device_id={a: lax.axis_index(a) + d for a, d in offs.items()},
            device_id_type=MESH,
        )

    def start(self):
        @pl.when(exists(self.offs))
        def _():
            self.copy.start()

    def wait_recv(self):
        @pl.when(exists(self.back))
        def _():
            self.copy.wait_recv()

    def wait_send(self):
        @pl.when(exists(self.offs))
        def _():
            self.copy.wait_send()


def enter():
    barrier = pltpu.get_barrier_semaphore()
    total = jnp.int32(0)
    offs = [{a: d} for a in NB for d in (-1, 1)]
    offs += [{"gy": i, "gz": j} for i in (-1, 1) for j in (-1, 1)]
    for o in offs:
        c = exists(o)

        @pl.when(c)
        def _():
            pl.semaphore_signal(
                barrier, inc=1, device_id={a: lax.axis_index(a) + d for a, d in o.items()}, device_id_type=MESH
            )

        total = total + c.astype(jnp.int32)
    return barrier, total


def lanes(shape):
    return lax.broadcasted_iota(jnp.int32, shape, len(shape) - 1)


def rows(shape):
    return lax.broadcasted_iota(jnp.int32, shape, len(shape) - 2)


def y_filter(ref, *at):
    acc = 7.0 * ref[(*at, pl.ds(8, Y))]
    for k in range(1, 7):
        acc = acc + (7.0 - k) * (ref[(*at, pl.ds(8 - k, Y))] + ref[(*at, pl.ds(8 + k, Y))])
    return acc


def y_local(v):
    def run(u):
        n = u.shape[0]
        two = u[: n - 1] + u[1:]
        three = two[: n - 2] + u[2:]
        four = three[: n - 3] + u[3:]
        return four[: n - 6] + three[4 : n - 2]

    zero = jnp.zeros((8, Z), jnp.float32)
    return run(run(jnp.concatenate([zero, v, zero], axis=0)[2:46]))


def x_run(ref, e, n, at):
    v = [ref[e + i, pl.ds(at, 8), :] for i in range(n + 12)]
    for _ in range(2):
        t = v[0]
        for u in v[1:7]:
            t = t + u
        out = [t]
        for i in range(7, len(v)):
            t = t + (v[i] - v[i - 7])
            out.append(t)
        v = out
    return v


def split(v):
    hi = v.astype(jnp.bfloat16)
    lo = (v - hi.astype(jnp.float32)).astype(jnp.bfloat16)
    return jnp.concatenate([hi, lo], axis=0)


def times(v, mat):
    n = v.shape[0]
    r = jnp.dot(split(v), mat[...], preferred_element_type=jnp.float32)
    return r[:n] + r[n:]


def fill_mats(band, tips):
    def put(ref, dist):
        ref[...] = jnp.maximum(7 - dist, 0).astype(jnp.float32).astype(jnp.bfloat16)

    i, j = rows((Z, Z)), lanes((Z, Z))
    put(band, jnp.abs(i - j))
    i, j = rows((128, 128)), lanes((128, 128))
    same = i // 8 == j // 8
    put(tips.at[0], jnp.where(same, 8 + j - i, 9))
    put(tips.at[1], jnp.where(same, 8 + i - j, 9))


def pack_z(ref, xs, out, fresh):
    slot = lanes((Y, 128)) // 8
    for j in (0, 1):
        left = jnp.zeros((Y, 128), jnp.float32) if fresh else out[0, j]
        right = jnp.zeros((Y, 128), jnp.float32) if fresh else out[1, j]
        for x in xs:
            if x // 16 != j:
                continue
            s = x % 16
            a = ref[x, :, 0:128]
            b = ref[x, :, 128:256]
            a = a if s == 0 else pltpu.roll(a, 8 * s, 1)
            b = b if s == 15 else pltpu.roll(b, 8 * s + 8, 1)
            left = jnp.where(slot == s, a, left)
            right = jnp.where(slot == s, b, right)
        out[0, j] = left
        out[1, j] = right


def yz_local(ref, band, x0, n, put):
    v = times(jnp.concatenate([y_local(ref[x0 + i]) for i in range(n)], axis=0), band)
    for i in range(n):
        put(x0 + i, v[i * Y : (i + 1) * Y])


def z_strips(strips, tips, zy):
    for side in (0, 1):
        v = jnp.concatenate([y_filter(strips, side, j) for j in (0, 1)], axis=0)
        v = times(v, tips.at[side])
        for j in (0, 1):
            zy[side, j] = v[j * Y : (j + 1) * Y]


def y_faces(faces, band, x0, n):
    out = []
    row = rows((n, 8, Z))
    for side in (0, 1):
        t = faces[side, x0 : x0 + n]
        acc = None
        for k in range(1, 7):
            if side == 0:
                u = jnp.where(row < k, (7.0 - k) * pltpu.roll(t, k, 1), 0.0)
            else:
                u = jnp.where(row >= 8 - k, (7.0 - k) * pltpu.roll(t, 8 - k, 1), 0.0)
            acc = u if acc is None else acc + u
        out.append(acc.reshape(n * 8, Z))
    v = times(jnp.concatenate(out, axis=0), band)
    return v[: n * 8].reshape(n, 8, Z), v[n * 8 :].reshape(n, 8, Z)


def yz_halo(faces, zy, band, x0, n, old, put):
    lane = lanes((Y, 128))
    first, last = y_faces(faces, band, x0, n)
    for i in range(n):
        x = x0 + i
        s, j = x % 16, x // 16
        lo, hi = zy[0, j], zy[1, j]
        lo = lo if s == 0 else pltpu.roll(lo, 128 - 8 * s, 1)
        hi = hi if s == 15 else pltpu.roll(hi, 120 - 8 * s, 1)
        v = old(x) + jnp.concatenate([jnp.where(lane < 8, lo, 0.0), jnp.where(lane >= 120, hi, 0.0)], axis=1)
        put(x, jnp.concatenate([v[0:8] + first[i], v[8 : Y - 8], v[Y - 8 : Y] + last[i]], axis=0))


def y_up(v):
    return jnp.where(rows(v.shape) == Y - 1, 0.0, pltpu.roll(v, Y - 1, 0))


def y_dn(v):
    return jnp.where(rows(v.shape) == 0, 0.0, pltpu.roll(v, 1, 0))


def z_up(v):
    return jnp.where(lanes(v.shape) == Z - 1, 0.0, pltpu.roll(v, Z - 1, 1))


def z_dn(v):
    return jnp.where(lanes(v.shape) == 0, 0.0, pltpu.roll(v, 1, 1))


def kernel(
    den_h, kind_h, vel_h, adj_h, res, sen, yf2, zx2, band, tips,
    den, kind, vel, adj, zp, yf, zx, zy, zp2, filt, em, pw, alpha, grid,
    cxs, cxr, cys, cyr, czs, czr, send, recv, load,
):
    sems = (send, recv)
    ix, iy, iz = (lax.axis_index(a) for a in NB)
    loads = [
        pltpu.make_async_copy(den_h, den, load.at[0]),
        pltpu.make_async_copy(vel_h, vel, load.at[1]),
        pltpu.make_async_copy(adj_h, adj, load.at[2]),
        pltpu.make_async_copy(kind_h, kind, load.at[3]),
    ]
    barrier, total = enter()
    loads[0].start()

    f32 = jnp.float32

    @pl.when(ix == 0)
    def _():
        filt[0:6] = jnp.zeros((6, Y, Z), f32)
        pw[0:6] = jnp.zeros((6, Y, Z), f32)
        cxr[0] = jnp.zeros((4, Y, Z), f32)

    @pl.when(ix == NB["gx"] - 1)
    def _():
        filt[38:44] = jnp.zeros((6, Y, Z), f32)
        pw[38:44] = jnp.zeros((6, Y, Z), f32)
        cxr[1] = jnp.zeros((4, Y, Z), f32)

    for side, at in ((0, 0), (1, NB["gz"] - 1)):

        @pl.when(iz == at)
        def _():
            zx[side] = jnp.zeros((2, 48, 128), f32)
            zx2[side] = jnp.zeros((2, 48, 128), f32)
            czr[side] = jnp.zeros((Y, 128), f32)

    for side, at in ((0, 0), (1, NB["gy"] - 1)):

        @pl.when(iy == at)
        def _():
            for r in (zx, zx2):
                r[:, :, pl.ds(40 * side, 8), :] = jnp.zeros((2, 2, 8, 128), f32)
            for r in (yf, yf2):
                r[side] = jnp.zeros((X, 8, Z), f32)
            cyr[side] = jnp.zeros((4, X, Z), f32)

    fill_mats(band, tips)

    def face_messages(name, src, faces, parts):
        out = []
        for p in parts:
            lo, hi = PARTS[p]
            xs = pl.ds(lo, hi - lo)
            out += [
                Msg(sems, f"{name}y0{p}", {"gy": -1}, src.at[xs, 0:6, :], faces.at[1, xs, 0:6, :]),
                Msg(sems, f"{name}y1{p}", {"gy": 1}, src.at[xs, Y - 6 : Y, :], faces.at[0, xs, 2:8, :]),
            ]
        return out

    def strip_messages(name, packed, strips):
        out = []
        for a, (d, mine, there) in enumerate(((-1, 0, 40), (1, 26, 2))):
            for b, e in enumerate((-1, 1)):
                out.append(
                    Msg(
                        sems, f"{name}d{a}{b}", {"gy": d, "gz": e},
                        packed.at[b, :, pl.ds(mine, 6), :], strips.at[1 - b, :, pl.ds(there, 6), :],
                    )
                )
        return out + [
            Msg(sems, f"{name}z0", {"gz": -1}, packed.at[0], strips.at[1, :, pl.ds(8, Y), :]),
            Msg(sems, f"{name}z1", {"gz": 1}, packed.at[1], strips.at[0, :, pl.ds(8, Y), :]),
        ]

    loads[0].wait()
    for c in loads[1:]:
        c.start()
    pack_z(den, range(X), zp, True)
    pl.semaphore_wait(barrier, total)
    msg_an = face_messages("a", den_h, yf, "lh")
    msg_az = strip_messages("a", zp, zx)
    msg_am = face_messages("a", den_h, yf, "m")
    for m in msg_az + msg_an + msg_am:
        m.start()

    def put_filt(x, v):
        filt[x + 6] = v

    def old_filt(x):
        return filt[x + 6]

    for x0, n in ((0, 6), (26, 6), (6, 10), (16, 10)):
        yz_local(den, band, x0, n, put_filt)
    for c in loads[1:]:
        c.wait()

    for side, x, sign in ((0, 0, 0.5), (1, X - 1, -0.5)):
        w = [adj[d, x] + 2.0 * vel[d, x] for d in range(3)]
        cxs[side, 0] = -(w[0] + sign * adj[3, x])
        cxs[side, 1] = -w[1]
        cxs[side, 2] = -w[2]
        cxs[side, 3] = -sign * adj[0, x]
    msg_f = [
        Msg(sems, "fx0", {"gx": -1}, cxs.at[0], cxr.at[1]),
        Msg(sems, "fx1", {"gx": 1}, cxs.at[1], cxr.at[0]),
        Msg(sems, "fy0", {"gy": -1}, cys.at[0], cyr.at[1]),
        Msg(sems, "fy1", {"gy": 1}, cys.at[1], cyr.at[0]),
        Msg(sems, "fz0", {"gz": -1}, czs.at[0], czr.at[1]),
        Msg(sems, "fz1", {"gz": 1}, czs.at[1], czr.at[0]),
    ]


    def y_ends(x, carry):
        for side, part, at, sign in ((0, pl.ds(0, 8), 0, 0.5), (1, pl.ds(Y - 8, 8), 7, -0.5)):
            w = [adj[d, x, part] + 2.0 * vel[d, x, part] for d in range(3)]
            out = (-w[0], -(w[1] + sign * adj[3, x, part]), -w[2], -sign * adj[1, x, part])
            for c in range(4):
                cys[side, c, pl.ds(x, 1)] = out[c][at : at + 1]
        return carry

    lax.fori_loop(0, X, y_ends, 0, unroll=4)

    def energy(x, carry):
        e = None
        for d in range(3):
            u = vel[d, x]
            t = u * (u + adj[d, x])
            e = t if e is None else e + t
        em[x] = jnp.where(kind[x] == 0, e, 0.0)
        return carry

    lax.fori_loop(0, X, energy, 0, unroll=4)

    for m in msg_f[2:4]:
        m.start()

    lane = lanes((Y, 128))

    def stencil(x, carry, lower, upper):
        to_prev, to_next = carry
        lam = [adj[d, x] for d in range(3)]
        mu2 = adj[3, x] * 0.5
        w = [lam[d] + 2.0 * vel[d, x] for d in range(3)]
        plus = [w[d] + mu2 for d in range(3)]
        minus = [w[d] - mu2 for d in range(3)]

        def at(d, q):
            return adj[d, q] + 2.0 * vel[d, q]

        out = []
        for d in range(3):
            t = y_up(plus[1] if d == 1 else w[d]) + y_dn(minus[1] if d == 1 else w[d])
            t = t + z_up(plus[2] if d == 2 else w[d]) + z_dn(minus[2] if d == 2 else w[d])
            if lower:
                t = t + at(d, x - 1)
                if d == 0:
                    t = t - 0.5 * adj[3, x - 1]
            if upper:
                t = t + at(d, x + 1)
                if d == 0:
                    t = t + 0.5 * adj[3, x + 1]
            out.append(-t)
        div = y_up(lam[1]) - y_dn(lam[1]) + z_up(lam[2]) - z_dn(lam[2])
        if upper:
            div = div + adj[0, x + 1]
        if lower:
            div = div - adj[0, x - 1]
        out.append(-0.5 * div)
        for c in range(4):
            res[c, x] = out[c]

        zs0 = (-w[0], -w[1], -plus[2], -0.5 * lam[2])
        zs1 = (-w[0], -w[1], -minus[2], 0.5 * lam[2])
        for c in range(4):
            at_lane = c * X + x
            first = pltpu.roll(zs0[c][:, 0:128], at_lane, 1)
            last = pltpu.roll(zs1[c][:, 128:256], lax.rem(at_lane + 1, 128), 1)
            to_prev = jnp.where(lane == at_lane, first, to_prev)
            to_next = jnp.where(lane == at_lane, last, to_next)
        return to_prev, to_next

    ends = (jnp.zeros((Y, 128), f32), jnp.zeros((Y, 128), f32))
    ends = stencil(0, ends, False, True)
    ends = lax.fori_loop(1, 10, lambda x, c: stencil(x, c, True, True), ends, unroll=3)

    for m in msg_an + msg_az:
        m.wait_recv()
    z_strips(zx, tips, zy)

    def x_messages(name, ref):
        out = []
        for k in range(3):
            out.append([
                Msg(sems, f"{name}{k}0", {"gx": -1}, ref.at[pl.ds(6 + 2 * k, 2)], ref.at[pl.ds(38 + 2 * k, 2)]),
                Msg(sems, f"{name}{k}1", {"gx": 1}, ref.at[pl.ds(36 - 2 * k, 2)], ref.at[pl.ds(4 - 2 * k, 2)]),
            ])
        return out

    msg_b = x_messages("b", filt)
    for x0 in (0, 26):
        yz_halo(yf, zy, band, x0, 6, old_filt, put_filt)
    for ms in msg_b:
        for m in ms:
            m.start()
    for m in msg_am:
        m.wait_recv()
    for x0 in (6, 16):
        yz_halo(yf, zy, band, x0, 10, old_filt, put_filt)

    def project(x, n):
        def strip(q, carry):
            at = pl.multiple_of(q * 8, 8)
            for i, f in enumerate(x_run(filt, x, n, at)):
                t = jnp.tanh(f * (4.0 * CUBE) - 2.0)
                r = 1.0 / (1.0 + (TANH2 + t) * (0.5 / TANH2))
                here = (x + i, pl.ds(at, 8))
                pw[x + i + 6, pl.ds(at, 8)] = (-8.0 / TANH2) * (r * r) * (1.0 - t * t) * em[here]
                k = kind[here]
                alpha[here] = jnp.where(k == 0, 4.0 * r - 2.0, jnp.where(k == 1, 2.0, 0.0))
            return carry

        lax.fori_loop(0, Y // 8, strip, 0, unroll=2)

    def smooth_x(x, n):
        def strip(q, carry):
            at = pl.multiple_of(q * 8, 8)
            for i, f in enumerate(x_run(pw, x, n, at)):
                grid[x + i, pl.ds(at, 8)] = f
            return carry

        lax.fori_loop(0, Y // 8, strip, 0, unroll=2)

    def put_sen(x, v):
        sen[x] = v

    for x in (6, 16):
        project(x, 10)

    ends = lax.fori_loop(10, X - 1, lambda x, c: stencil(x, c, True, True), ends, unroll=3)
    ends = stencil(X - 1, ends, True, False)
    czs[0], czs[1] = ends
    for m in msg_f[4:]:
        m.start()

    msg_c = x_messages("c", pw)
    for k in range(3):
        for m in msg_b[k]:
            m.wait_recv()
        for x in (4 - 2 * k, 26 + 2 * k):
            project(x, 2)
        for m in msg_c[2 - k]:
            m.start()

    for x in (6, 16):
        smooth_x(x, 10)
    pack_z(grid, range(6, 26), zp2, True)
    for x0 in (6, 16):
        yz_local(grid, band, x0, 10, put_sen)
    msg_dm = face_messages("d", grid, yf2, "m")
    for m in msg_dm:
        m.start()
    for m in msg_f[:2]:
        m.start()

    for m in msg_f[2:]:
        m.wait_recv()

    def finish(x, carry):
        a = alpha[x] + 6.0
        k = kind[x]
        row = rows((8, Z))
        for c in range(4):
            at_lane = c * X + x
            first = pltpu.roll(czr[0], (128 - at_lane) % 128, 1)
            last = pltpu.roll(czr[1], 127 - at_lane, 1)
            top = jnp.where(row == 0, cyr[0, c, pl.ds(x, 1)], 0.0)
            end = jnp.where(row == 7, cyr[1, c, pl.ds(x, 1)], 0.0)
            r = res[c, x]
            r = jnp.concatenate([r[0:8] + top, r[8 : Y - 8], r[Y - 8 : Y] + end], axis=0)
            r = r + jnp.concatenate([jnp.where(lane == 0, first, 0.0), jnp.where(lane == 127, last, 0.0)], axis=1)
            v = adj[c, x]
            if c < 3:
                res[c, x] = jnp.where(k == 2, v, r + a * (v + 2.0 * vel[c, x]))
            else:
                res[c, x] = jnp.where(k == 3, v, r)
        return carry

    lax.fori_loop(1, 13, finish, 0, unroll=3)

    for ms in msg_c:
        for m in ms:
            m.wait_recv()
    for x in (0, 26):
        smooth_x(x, 6)

    pack_z(grid, (*range(0, 6), *range(26, 32)), zp2, False)
    msg_dz = strip_messages("d", zp2, zx2)
    msg_dn = face_messages("d", grid, yf2, "lh")
    for m in msg_dz + msg_dn:
        m.start()
    for x0 in (0, 26):
        yz_local(grid, band, x0, 6, put_sen)

    lax.fori_loop(13, X - 1, finish, 0, unroll=3)
    for m in msg_f[:2]:
        m.wait_recv()
    for side, x in ((0, 0), (1, X - 1)):
        for c in range(4):
            res[c, x] += cxr[side, c]
        finish(x, 0)

    for m in msg_an + msg_am + msg_az + sum(msg_b + msg_c, []) + msg_f:
        m.wait_send()
    for m in msg_dm + msg_dn + msg_dz:
        m.wait_recv()
    for m in msg_dm + msg_dn + msg_dz:
        m.wait_send()


def finish_kernel(res, sen_in, yf2, zx2, band, tips, res_o, sen_o, zy, sen, sems):
    out_r = pltpu.make_async_copy(res, res_o, sems.at[0])
    out_r.start()
    z_strips(zx2, tips, zy)

    def old(x):
        return sen_in[x]

    def put(x, v):
        sen[x] = v * CUBE

    out_s = []
    for g in range(4):
        yz_halo(yf2, zy, band, g * 8, 8, old, put)
        part = pl.ds(g * 8, 8)
        out_s.append(pltpu.make_async_copy(sen.at[part], sen_o.at[part], sems.at[1 + g]))
        out_s[-1].start()
    out_r.wait()
    for c in out_s:
        c.wait()


def body(*args):
    f32 = jnp.float32
    block = (X, Y, Z)
    strips, wide = (2, 2, Y, 128), (2, 2, 48, 128)
    vmem = pl.BlockSpec(memory_space=pltpu.VMEM)
    near = pl.pallas_call(
        kernel,
        out_shape=(
            pltpu.VMEM((4, *block), f32),
            pltpu.VMEM(block, f32),
            pltpu.VMEM((2, X, 8, Z), f32),
            pltpu.VMEM(wide, f32),
            pltpu.VMEM((Z, Z), jnp.bfloat16),
            pltpu.VMEM((2, 128, 128), jnp.bfloat16),
        ),
        in_specs=[pl.BlockSpec(memory_space=pl.ANY)] * 4,
        out_specs=(vmem,) * 6,
        scratch_shapes=[
            pltpu.VMEM(block, f32),
            pltpu.VMEM(block, jnp.int32),
            pltpu.VMEM((3, *block), f32),
            pltpu.VMEM((4, *block), f32),
            pltpu.VMEM(strips, f32),
            pltpu.VMEM((2, X, 8, Z), f32),
            pltpu.VMEM(wide, f32),
            pltpu.VMEM(strips, f32),
            pltpu.VMEM(strips, f32),
            pltpu.VMEM((44, Y, Z), f32),
            pltpu.VMEM(block, f32),
            pltpu.VMEM((44, Y, Z), f32),
            pltpu.VMEM(block, f32),
            pltpu.VMEM(block, f32),
            pltpu.VMEM((2, 4, Y, Z), f32),
            pltpu.VMEM((2, 4, Y, Z), f32),
            pltpu.VMEM((2, 4, X, Z), f32),
            pltpu.VMEM((2, 4, X, Z), f32),
            pltpu.VMEM((2, Y, 128), f32),
            pltpu.VMEM((2, Y, 128), f32),
            pltpu.SemaphoreType.DMA((len(NAMES),)),
            pltpu.SemaphoreType.DMA((len(NAMES),)),
            pltpu.SemaphoreType.DMA((4,)),
        ],
        compiler_params=pltpu.CompilerParams(
            collective_id=0, has_side_effects=True, vmem_limit_bytes=32 * 2**20
        ),
    )(*(pltpu.with_memory_space_constraint(a, pltpu.HBM) for a in args))
    return pl.pallas_call(
        finish_kernel,
        out_shape=(jax.ShapeDtypeStruct((4, *block), f32), jax.ShapeDtypeStruct(block, f32)),
        in_specs=[vmem] * 6,
        out_specs=(pl.BlockSpec(memory_space=pl.ANY),) * 2,
        scratch_shapes=[
            pltpu.VMEM(strips, f32),
            pltpu.VMEM(block, f32),
            pltpu.SemaphoreType.DMA((5,)),
        ],
        compiler_params=pltpu.CompilerParams(vmem_limit_bytes=16 * 2**20),
    )(*near)


def solution(mesh):
    own = P("gx", "gy", "gz")
    fields = P(None, "gx", "gy", "gz")
    return jax.shard_map(
        body, mesh=mesh, in_specs=(own, own, fields, fields), out_specs=(fields, own), check_vma=False
    )
```

```python
import math

import jax
import jax.numpy as jnp
from jax import lax
from jax.experimental import pallas as pl
from jax.experimental.pallas import tpu as pltpu
from jax.sharding import PartitionSpec as P

MESH = pl.DeviceIdType.MESH
NB = {"gx": 8, "gy": 4, "gz": 8}
X, Y, Z = 32, 32, 256
TANH2 = math.tanh(2.0)
CUBE = 1.0 / (49.0**3)

NAMES = (
    [f"{k}y{i}{part}" for k in "ad" for i in (0, 1) for part in "lhm"]
    + [f"{k}z{i}" for k in "ad" for i in (0, 1)]
    + [f"{k}d{i}{j}" for k in "ad" for i in (0, 1) for j in (0, 1)]
    + [f"{c}{k}{i}" for c in "bc" for k in range(3) for i in (0, 1)]
    + [f"f{c}{i}" for c in "xyz" for i in (0, 1)]
)
PARTS = {"l": (0, 6), "h": (26, 32), "m": (6, 26)}
SLOT = {n: i for i, n in enumerate(NAMES)}


def exists(offs):
    ok = None
    for axis, d in offs.items():
        i = lax.axis_index(axis)
        c = (i > 0) if d < 0 else (i < NB[axis] - 1)
        ok = c if ok is None else jnp.logical_and(ok, c)
    return ok


class Msg:
    def __init__(self, sems, name, offs, src, dst):
        self.offs = offs
        self.back = {a: -d for a, d in offs.items()}
        k = SLOT[name]
        self.copy = pltpu.make_async_remote_copy(
            src_ref=src,
            dst_ref=dst,
            send_sem=sems[0].at[k],
            recv_sem=sems[1].at[k],
            device_id={a: lax.axis_index(a) + d for a, d in offs.items()},
            device_id_type=MESH,
        )

    def start(self):
        @pl.when(exists(self.offs))
        def _():
            self.copy.start()

    def wait_recv(self):
        @pl.when(exists(self.back))
        def _():
            self.copy.wait_recv()

    def wait_send(self):
        @pl.when(exists(self.offs))
        def _():
            self.copy.wait_send()


def enter():
    barrier = pltpu.get_barrier_semaphore()
    total = jnp.int32(0)
    offs = [{a: d} for a in NB for d in (-1, 1)]
    offs += [{"gy": i, "gz": j} for i in (-1, 1) for j in (-1, 1)]
    for o in offs:
        c = exists(o)

        @pl.when(c)
        def _():
            pl.semaphore_signal(
                barrier, inc=1, device_id={a: lax.axis_index(a) + d for a, d in o.items()}, device_id_type=MESH
            )

        total = total + c.astype(jnp.int32)
    return barrier, total


def lanes(shape):
    return lax.broadcasted_iota(jnp.int32, shape, len(shape) - 1)


def rows(shape):
    return lax.broadcasted_iota(jnp.int32, shape, len(shape) - 2)


def y_filter(ref, *at):
    acc = 7.0 * ref[(*at, pl.ds(8, Y))]
    for k in range(1, 7):
        acc = acc + (7.0 - k) * (ref[(*at, pl.ds(8 - k, Y))] + ref[(*at, pl.ds(8 + k, Y))])
    return acc


def y_local(v):
    def run(u):
        n = u.shape[0]
        two = u[: n - 1] + u[1:]
        three = two[: n - 2] + u[2:]
        four = three[: n - 3] + u[3:]
        return four[: n - 6] + three[4 : n - 2]

    zero = jnp.zeros((8, Z), jnp.float32)
    return run(run(jnp.concatenate([zero, v, zero], axis=0)[2:46]))


def x_run(ref, e, n, at):
    v = [ref[e + i, pl.ds(at, 8), :] for i in range(n + 12)]
    for _ in range(2):
        t = v[0]
        for u in v[1:7]:
            t = t + u
        out = [t]
        for i in range(7, len(v)):
            t = t + (v[i] - v[i - 7])
            out.append(t)
        v = out
    return v


def split(v):
    hi = v.astype(jnp.bfloat16)
    lo = (v - hi.astype(jnp.float32)).astype(jnp.bfloat16)
    return jnp.concatenate([hi, lo], axis=0)


def times(v, mat):
    n = v.shape[0]
    r = jnp.dot(split(v), mat[...], preferred_element_type=jnp.float32)
    return r[:n] + r[n:]


def fill_mats(band, tips):
    def put(ref, dist):
        ref[...] = jnp.maximum(7 - dist, 0).astype(jnp.float32).astype(jnp.bfloat16)

    i, j = rows((Z, Z)), lanes((Z, Z))
    put(band, jnp.abs(i - j))
    i, j = rows((128, 128)), lanes((128, 128))
    same = i // 8 == j // 8
    put(tips.at[0], jnp.where(same, 8 + j - i, 9))
    put(tips.at[1], jnp.where(same, 8 + i - j, 9))


def pack_z(ref, xs, out, fresh):
    slot = lanes((Y, 128)) // 8
    for j in (0, 1):
        left = jnp.zeros((Y, 128), jnp.float32) if fresh else out[0, j]
        right = jnp.zeros((Y, 128), jnp.float32) if fresh else out[1, j]
        for x in xs:
            if x // 16 != j:
                continue
            s = x % 16
            a = ref[x, :, 0:128]
            b = ref[x, :, 128:256]
            a = a if s == 0 else pltpu.roll(a, 8 * s, 1)
            b = b if s == 15 else pltpu.roll(b, 8 * s + 8, 1)
            left = jnp.where(slot == s, a, left)
            right = jnp.where(slot == s, b, right)
        out[0, j] = left
        out[1, j] = right


def yz_local(ref, band, x0, n, put):
    v = times(jnp.concatenate([y_local(ref[x0 + i]) for i in range(n)], axis=0), band)
    for i in range(n):
        put(x0 + i, v[i * Y : (i + 1) * Y])


def z_strips(strips, tips, zy):
    for side in (0, 1):
        v = jnp.concatenate([y_filter(strips, side, j) for j in (0, 1)], axis=0)
        v = times(v, tips.at[side])
        for j in (0, 1):
            zy[side, j] = v[j * Y : (j + 1) * Y]


def y_faces(faces, band, x0, n):
    out = []
    row = rows((n, 8, Z))
    for side in (0, 1):
        t = faces[side, x0 : x0 + n]
        acc = None
        for k in range(1, 7):
            if side == 0:
                u = jnp.where(row < k, (7.0 - k) * pltpu.roll(t, k, 1), 0.0)
            else:
                u = jnp.where(row >= 8 - k, (7.0 - k) * pltpu.roll(t, 8 - k, 1), 0.0)
            acc = u if acc is None else acc + u
        out.append(acc.reshape(n * 8, Z))
    v = times(jnp.concatenate(out, axis=0), band)
    return v[: n * 8].reshape(n, 8, Z), v[n * 8 :].reshape(n, 8, Z)


def yz_halo(faces, zy, band, x0, n, old, put):
    lane = lanes((Y, 128))
    first, last = y_faces(faces, band, x0, n)
    for i in range(n):
        x = x0 + i
        s, j = x % 16, x // 16
        lo, hi = zy[0, j], zy[1, j]
        lo = lo if s == 0 else pltpu.roll(lo, 128 - 8 * s, 1)
        hi = hi if s == 15 else pltpu.roll(hi, 120 - 8 * s, 1)
        v = old(x) + jnp.concatenate([jnp.where(lane < 8, lo, 0.0), jnp.where(lane >= 120, hi, 0.0)], axis=1)
        put(x, jnp.concatenate([v[0:8] + first[i], v[8 : Y - 8], v[Y - 8 : Y] + last[i]], axis=0))


def y_up(v):
    return jnp.where(rows(v.shape) == Y - 1, 0.0, pltpu.roll(v, Y - 1, 0))


def y_dn(v):
    return jnp.where(rows(v.shape) == 0, 0.0, pltpu.roll(v, 1, 0))


def z_up(v):
    return jnp.where(lanes(v.shape) == Z - 1, 0.0, pltpu.roll(v, Z - 1, 1))


def z_dn(v):
    return jnp.where(lanes(v.shape) == 0, 0.0, pltpu.roll(v, 1, 1))


def kernel(
    den_h, kind_h, vel_h, adj_h, res, sen, yf2, zx2, band, tips,
    den, kind, vel, adj, zp, yf, zx, zy, zp2, filt, em, pw, alpha, grid,
    cxs, cxr, cys, cyr, czs, czr, send, recv, load,
):
    sems = (send, recv)
    ix, iy, iz = (lax.axis_index(a) for a in NB)
    loads = [
        pltpu.make_async_copy(den_h, den, load.at[0]),
        pltpu.make_async_copy(vel_h, vel, load.at[1]),
        pltpu.make_async_copy(adj_h, adj, load.at[2]),
        pltpu.make_async_copy(kind_h, kind, load.at[3]),
    ]
    barrier, total = enter()
    loads[0].start()

    f32 = jnp.float32

    @pl.when(ix == 0)
    def _():
        filt[0:6] = jnp.zeros((6, Y, Z), f32)
        pw[0:6] = jnp.zeros((6, Y, Z), f32)
        cxr[0] = jnp.zeros((4, Y, Z), f32)

    @pl.when(ix == NB["gx"] - 1)
    def _():
        filt[38:44] = jnp.zeros((6, Y, Z), f32)
        pw[38:44] = jnp.zeros((6, Y, Z), f32)
        cxr[1] = jnp.zeros((4, Y, Z), f32)

    for side, at in ((0, 0), (1, NB["gz"] - 1)):

        @pl.when(iz == at)
        def _():
            zx[side] = jnp.zeros((2, 48, 128), f32)
            zx2[side] = jnp.zeros((2, 48, 128), f32)
            czr[side] = jnp.zeros((Y, 128), f32)

    for side, at in ((0, 0), (1, NB["gy"] - 1)):

        @pl.when(iy == at)
        def _():
            for r in (zx, zx2):
                r[:, :, pl.ds(40 * side, 8), :] = jnp.zeros((2, 2, 8, 128), f32)
            for r in (yf, yf2):
                r[side] = jnp.zeros((X, 8, Z), f32)
            cyr[side] = jnp.zeros((4, X, Z), f32)

    fill_mats(band, tips)

    def face_messages(name, src, faces, parts):
        out = []
        for p in parts:
            lo, hi = PARTS[p]
            xs = pl.ds(lo, hi - lo)
            out += [
                Msg(sems, f"{name}y0{p}", {"gy": -1}, src.at[xs, 0:6, :], faces.at[1, xs, 0:6, :]),
                Msg(sems, f"{name}y1{p}", {"gy": 1}, src.at[xs, Y - 6 : Y, :], faces.at[0, xs, 2:8, :]),
            ]
        return out

    def strip_messages(name, packed, strips):
        out = []
        for a, (d, mine, there) in enumerate(((-1, 0, 40), (1, 26, 2))):
            for b, e in enumerate((-1, 1)):
                out.append(
                    Msg(
                        sems, f"{name}d{a}{b}", {"gy": d, "gz": e},
                        packed.at[b, :, pl.ds(mine, 6), :], strips.at[1 - b, :, pl.ds(there, 6), :],
                    )
                )
        return out + [
            Msg(sems, f"{name}z0", {"gz": -1}, packed.at[0], strips.at[1, :, pl.ds(8, Y), :]),
            Msg(sems, f"{name}z1", {"gz": 1}, packed.at[1], strips.at[0, :, pl.ds(8, Y), :]),
        ]

    loads[0].wait()
    for c in loads[1:]:
        c.start()
    pack_z(den, range(X), zp, True)
    pl.semaphore_wait(barrier, total)
    msg_an = face_messages("a", den_h, yf, "lh")
    msg_az = strip_messages("a", zp, zx)
    msg_am = face_messages("a", den_h, yf, "m")
    for m in msg_az + msg_an + msg_am:
        m.start()

    def put_filt(x, v):
        filt[x + 6] = v

    def old_filt(x):
        return filt[x + 6]

    for x0, n in ((0, 6), (26, 6), (6, 10), (16, 10)):
        yz_local(den, band, x0, n, put_filt)
    for c in loads[1:]:
        c.wait()

    for side, x, sign in ((0, 0, 0.5), (1, X - 1, -0.5)):
        w = [adj[d, x] + 2.0 * vel[d, x] for d in range(3)]
        cxs[side, 0] = -(w[0] + sign * adj[3, x])
        cxs[side, 1] = -w[1]
        cxs[side, 2] = -w[2]
        cxs[side, 3] = -sign * adj[0, x]
    msg_f = [
        Msg(sems, "fx0", {"gx": -1}, cxs.at[0], cxr.at[1]),
        Msg(sems, "fx1", {"gx": 1}, cxs.at[1], cxr.at[0]),
        Msg(sems, "fy0", {"gy": -1}, cys.at[0], cyr.at[1]),
        Msg(sems, "fy1", {"gy": 1}, cys.at[1], cyr.at[0]),
        Msg(sems, "fz0", {"gz": -1}, czs.at[0], czr.at[1]),
        Msg(sems, "fz1", {"gz": 1}, czs.at[1], czr.at[0]),
    ]


    def y_ends(x, carry):
        for side, part, at, sign in ((0, pl.ds(0, 8), 0, 0.5), (1, pl.ds(Y - 8, 8), 7, -0.5)):
            w = [adj[d, x, part] + 2.0 * vel[d, x, part] for d in range(3)]
            out = (-w[0], -(w[1] + sign * adj[3, x, part]), -w[2], -sign * adj[1, x, part])
            for c in range(4):
                cys[side, c, pl.ds(x, 1)] = out[c][at : at + 1]
        return carry

    lax.fori_loop(0, X, y_ends, 0, unroll=4)

    def energy(x, carry):
        e = None
        for d in range(3):
            u = vel[d, x]
            t = u * (u + adj[d, x])
            e = t if e is None else e + t
        em[x] = jnp.where(kind[x] == 0, e, 0.0)
        return carry

    lax.fori_loop(0, X, energy, 0, unroll=4)

    for m in msg_f[2:4]:
        m.start()

    lane = lanes((Y, 128))

    def stencil(x, carry, lower, upper):
        to_prev, to_next = carry
        lam = [adj[d, x] for d in range(3)]
        mu2 = adj[3, x] * 0.5
        w = [lam[d] + 2.0 * vel[d, x] for d in range(3)]
        plus = [w[d] + mu2 for d in range(3)]
        minus = [w[d] - mu2 for d in range(3)]

        def at(d, q):
            return adj[d, q] + 2.0 * vel[d, q]

        out = []
        for d in range(3):
            t = y_up(plus[1] if d == 1 else w[d]) + y_dn(minus[1] if d == 1 else w[d])
            t = t + z_up(plus[2] if d == 2 else w[d]) + z_dn(minus[2] if d == 2 else w[d])
            if lower:
                t = t + at(d, x - 1)
                if d == 0:
                    t = t - 0.5 * adj[3, x - 1]
            if upper:
                t = t + at(d, x + 1)
                if d == 0:
                    t = t + 0.5 * adj[3, x + 1]
            out.append(-t)
        div = y_up(lam[1]) - y_dn(lam[1]) + z_up(lam[2]) - z_dn(lam[2])
        if upper:
            div = div + adj[0, x + 1]
        if lower:
            div = div - adj[0, x - 1]
        out.append(-0.5 * div)
        for c in range(4):
            res[c, x] = out[c]

        zs0 = (-w[0], -w[1], -plus[2], -0.5 * lam[2])
        zs1 = (-w[0], -w[1], -minus[2], 0.5 * lam[2])
        for c in range(4):
            at_lane = c * X + x
            first = pltpu.roll(zs0[c][:, 0:128], at_lane, 1)
            last = pltpu.roll(zs1[c][:, 128:256], lax.rem(at_lane + 1, 128), 1)
            to_prev = jnp.where(lane == at_lane, first, to_prev)
            to_next = jnp.where(lane == at_lane, last, to_next)
        return to_prev, to_next

    ends = (jnp.zeros((Y, 128), f32), jnp.zeros((Y, 128), f32))
    ends = stencil(0, ends, False, True)
    ends = lax.fori_loop(1, 10, lambda x, c: stencil(x, c, True, True), ends, unroll=3)

    for m in msg_an + msg_az:
        m.wait_recv()
    z_strips(zx, tips, zy)

    def x_messages(name, ref):
        out = []
        for k in range(3):
            out.append([
                Msg(sems, f"{name}{k}0", {"gx": -1}, ref.at[pl.ds(6 + 2 * k, 2)], ref.at[pl.ds(38 + 2 * k, 2)]),
                Msg(sems, f"{name}{k}1", {"gx": 1}, ref.at[pl.ds(36 - 2 * k, 2)], ref.at[pl.ds(4 - 2 * k, 2)]),
            ])
        return out

    msg_b = x_messages("b", filt)
    for x0 in (0, 26):
        yz_halo(yf, zy, band, x0, 6, old_filt, put_filt)
    for ms in msg_b:
        for m in ms:
            m.start()
    for m in msg_am:
        m.wait_recv()
    for x0 in (6, 16):
        yz_halo(yf, zy, band, x0, 10, old_filt, put_filt)

    def project(x, n):
        def strip(q, carry):
            at = pl.multiple_of(q * 8, 8)
            for i, f in enumerate(x_run(filt, x, n, at)):
                t = jnp.tanh(f * (4.0 * CUBE) - 2.0)
                r = 1.0 / (1.0 + (TANH2 + t) * (0.5 / TANH2))
                here = (x + i, pl.ds(at, 8))
                pw[x + i + 6, pl.ds(at, 8)] = (-8.0 / TANH2) * (r * r) * (1.0 - t * t) * em[here]
                k = kind[here]
                alpha[here] = jnp.where(k == 0, 4.0 * r - 2.0, jnp.where(k == 1, 2.0, 0.0))
            return carry

        lax.fori_loop(0, Y // 8, strip, 0, unroll=2)

    def smooth_x(x, n):
        def strip(q, carry):
            at = pl.multiple_of(q * 8, 8)
            for i, f in enumerate(x_run(pw, x, n, at)):
                grid[x + i, pl.ds(at, 8)] = f
            return carry

        lax.fori_loop(0, Y // 8, strip, 0, unroll=2)

    def put_sen(x, v):
        sen[x] = v

    for x in (6, 16):
        project(x, 10)

    ends = lax.fori_loop(10, X - 1, lambda x, c: stencil(x, c, True, True), ends, unroll=3)
    ends = stencil(X - 1, ends, True, False)
    czs[0], czs[1] = ends
    for m in msg_f[4:]:
        m.start()

    msg_c = x_messages("c", pw)
    for k in range(3):
        for m in msg_b[k]:
            m.wait_recv()
        for x in (4 - 2 * k, 26 + 2 * k):
            project(x, 2)
        for m in msg_c[2 - k]:
            m.start()

    for x in (6, 16):
        smooth_x(x, 10)
    pack_z(grid, range(6, 26), zp2, True)
    for x0 in (6, 16):
        yz_local(grid, band, x0, 10, put_sen)
    for m in msg_f[:2]:
        m.start()

    for m in msg_f[2:]:
        m.wait_recv()

    def finish(x, carry):
        a = alpha[x] + 6.0
        k = kind[x]
        row = rows((8, Z))
        for c in range(4):
            at_lane = c * X + x
            first = pltpu.roll(czr[0], (128 - at_lane) % 128, 1)
            last = pltpu.roll(czr[1], 127 - at_lane, 1)
            top = jnp.where(row == 0, cyr[0, c, pl.ds(x, 1)], 0.0)
            end = jnp.where(row == 7, cyr[1, c, pl.ds(x, 1)], 0.0)
            r = res[c, x]
            r = jnp.concatenate([r[0:8] + top, r[8 : Y - 8], r[Y - 8 : Y] + end], axis=0)
            r = r + jnp.concatenate([jnp.where(lane == 0, first, 0.0), jnp.where(lane == 127, last, 0.0)], axis=1)
            v = adj[c, x]
            if c < 3:
                res[c, x] = jnp.where(k == 2, v, r + a * (v + 2.0 * vel[c, x]))
            else:
                res[c, x] = jnp.where(k == 3, v, r)
        return carry

    lax.fori_loop(1, 13, finish, 0, unroll=3)
    msg_dm = face_messages("d", grid, yf2, "m")
    for m in msg_dm:
        m.start()

    for ms in msg_c:
        for m in ms:
            m.wait_recv()
    for x in (0, 26):
        smooth_x(x, 6)

    pack_z(grid, (*range(0, 6), *range(26, 32)), zp2, False)
    msg_dz = strip_messages("d", zp2, zx2)
    msg_dn = face_messages("d", grid, yf2, "lh")
    for m in msg_dz + msg_dn:
        m.start()
    for x0 in (0, 26):
        yz_local(grid, band, x0, 6, put_sen)

    lax.fori_loop(13, X - 1, finish, 0, unroll=3)
    for m in msg_f[:2]:
        m.wait_recv()
    for side, x in ((0, 0), (1, X - 1)):
        for c in range(4):
            res[c, x] += cxr[side, c]
        finish(x, 0)

    for m in msg_an + msg_am + msg_az + sum(msg_b + msg_c, []) + msg_f:
        m.wait_send()
    for m in msg_dm + msg_dn + msg_dz:
        m.wait_recv()
    for m in msg_dm + msg_dn + msg_dz:
        m.wait_send()


def finish_kernel(res, sen_in, yf2, zx2, band, tips, res_o, sen_o, zy, sen, sems):
    out_r = pltpu.make_async_copy(res, res_o, sems.at[0])
    out_r.start()
    z_strips(zx2, tips, zy)

    def old(x):
        return sen_in[x]

    def put(x, v):
        sen[x] = v * CUBE

    out_s = []
    for g in range(4):
        yz_halo(yf2, zy, band, g * 8, 8, old, put)
        part = pl.ds(g * 8, 8)
        out_s.append(pltpu.make_async_copy(sen.at[part], sen_o.at[part], sems.at[1 + g]))
        out_s[-1].start()
    out_r.wait()
    for c in out_s:
        c.wait()


def body(*args):
    f32 = jnp.float32
    block = (X, Y, Z)
    strips, wide = (2, 2, Y, 128), (2, 2, 48, 128)
    vmem = pl.BlockSpec(memory_space=pltpu.VMEM)
    near = pl.pallas_call(
        kernel,
        out_shape=(
            pltpu.VMEM((4, *block), f32),
            pltpu.VMEM(block, f32),
            pltpu.VMEM((2, X, 8, Z), f32),
            pltpu.VMEM(wide, f32),
            pltpu.VMEM((Z, Z), jnp.bfloat16),
            pltpu.VMEM((2, 128, 128), jnp.bfloat16),
        ),
        in_specs=[pl.BlockSpec(memory_space=pl.ANY)] * 4,
        out_specs=(vmem,) * 6,
        scratch_shapes=[
            pltpu.VMEM(block, f32),
            pltpu.VMEM(block, jnp.int32),
            pltpu.VMEM((3, *block), f32),
            pltpu.VMEM((4, *block), f32),
            pltpu.VMEM(strips, f32),
            pltpu.VMEM((2, X, 8, Z), f32),
            pltpu.VMEM(wide, f32),
            pltpu.VMEM(strips, f32),
            pltpu.VMEM(strips, f32),
            pltpu.VMEM((44, Y, Z), f32),
            pltpu.VMEM(block, f32),
            pltpu.VMEM((44, Y, Z), f32),
            pltpu.VMEM(block, f32),
            pltpu.VMEM(block, f32),
            pltpu.VMEM((2, 4, Y, Z), f32),
            pltpu.VMEM((2, 4, Y, Z), f32),
            pltpu.VMEM((2, 4, X, Z), f32),
            pltpu.VMEM((2, 4, X, Z), f32),
            pltpu.VMEM((2, Y, 128), f32),
            pltpu.VMEM((2, Y, 128), f32),
            pltpu.SemaphoreType.DMA((len(NAMES),)),
            pltpu.SemaphoreType.DMA((len(NAMES),)),
            pltpu.SemaphoreType.DMA((4,)),
        ],
        compiler_params=pltpu.CompilerParams(
            collective_id=0, has_side_effects=True, vmem_limit_bytes=32 * 2**20
        ),
    )(*(pltpu.with_memory_space_constraint(a, pltpu.HBM) for a in args))
    return pl.pallas_call(
        finish_kernel,
        out_shape=(jax.ShapeDtypeStruct((4, *block), f32), jax.ShapeDtypeStruct(block, f32)),
        in_specs=[vmem] * 6,
        out_specs=(pl.BlockSpec(memory_space=pl.ANY),) * 2,
        scratch_shapes=[
            pltpu.VMEM(strips, f32),
            pltpu.VMEM(block, f32),
            pltpu.SemaphoreType.DMA((5,)),
        ],
        compiler_params=pltpu.CompilerParams(vmem_limit_bytes=16 * 2**20),
    )(*near)


def solution(mesh):
    own = P("gx", "gy", "gz")
    fields = P(None, "gx", "gy", "gz")
    return jax.shard_map(
        body, mesh=mesh, in_specs=(own, own, fields, fields), out_specs=(fields, own), check_vma=False
    )
```
